128 devices in a mesh: dom: 64 (over x_hi, y, z, core), band: 2 (over x_lo).
Axes of the slice: x: 4 (x_hi: 2, x_lo: 2; x = x_hi * 2 + x_lo), y: 4, z: 4, core: 2. Of those that a mesh axis runs over, the one named last changes fastest.
Arguments:
- states: bfloat16 [1051392, 256], P('dom', 'band'), may hold values from -6 to 6
- mass_scale: float32 [1051392], P('dom'), may hold values from 0.5 to 2
- potential: float32 [64, 36864], P(None, 'dom'), may hold values from -6 to 6
- kinetic: bfloat16 [64, 64], replicated, may hold values from -0.75 to 0.75
- basis_fn: bfloat16 [64, 64], replicated, may hold values from -0.75 to 0.75
- connectivity: int32 [64, 36864], P(None, 'dom'), may hold values from 0 to 17796, as said below
- boundary: int32 [87616], P('dom'), may hold values from 0 to 16427, as said below
- owners: int32 [8, 8], replicated, may hold values from 0 to 63, as said below
Outputs:
- filtered: bfloat16 [1051392, 256], P('dom', 'band')
- projected: float32 [256, 2, 2, 1024], P('dom', 'band')
The draws below stay inside these ranges and needn't reach their ends.
Inputs may be any that keep to these rules, and one draw needn't show every extreme that they name: `connectivity`: entries below 16428 are distinct owned nodes of the cell's domain; the others name the plane of the domain above. `boundary`: each domain's 1369 entries are distinct local node numbers. `owners`: in every column block of tiles no domain owns more than 4 tiles, and some domain owns exactly 4.
All inputs are finite; a program needn't handle non-finite values.
Results may differ from the reference program's by a relative error of at most 0.015.
Values may be sent and summed in bfloat16 or wider, within the bound.
No kernel may reach another device: no remote copies, remote signals or barrier semaphores. Data moves between devices by JAX's collectives and lax.ppermute only.
A program may use at most 128 MiB of HBM per device.

```python
import math
import jax
import jax.numpy as jnp
from jax import lax

NPC = 64
QP = 64
TILE = 32
CAP = 4
CX = 4
CY = 12
CZ = 12
PLANE = 1369
NODE_DEV = 16428
CELLS_DEV = 576
NODES = 1051392
CELLS = 36864
NS = 256
NT = 8
CB = 4
TB = 32
N_DOM = 64
N_BAND = 2


def node_orders(key):
    keys = jax.vmap(lambda d: jax.random.fold_in(key, d))(jnp.arange(N_DOM))
    return jax.vmap(lambda k: jax.random.permutation(k, NODE_DEV))(keys).astype(jnp.int32)


def draw_connectivity(key, part):
    orders = node_orders(key)
    cell_ids = jnp.arange(CX * CY * CZ, dtype=jnp.int32)
    cell_x = cell_ids // (CY * CZ)
    cell_y = cell_ids // CZ % CY
    cell_z = cell_ids % CZ
    local = jnp.arange(NPC, dtype=jnp.int32)
    plane_x = 3 * cell_x[None, :] + (local // 16)[:, None]
    plane_y = 3 * cell_y[None, :] + (local // 4 % 4)[:, None]
    plane_z = 3 * cell_z[None, :] + (local % 4)[:, None]
    inplane = plane_y * (3 * CZ + 1) + plane_z
    canonical = jnp.minimum(plane_x * PLANE + inplane, NODE_DEV - 1)

    def per_domain(order):
        return jnp.where(plane_x == 3 * CX, NODE_DEV + inplane, order[canonical])
    table = jax.vmap(per_domain)(orders)
    return table.transpose(1, 0, 2).reshape(NPC, N_DOM * CX * CY * CZ).astype(jnp.int32)


def draw_boundary(key, part):
    orders = node_orders(key)
    return orders[:, :PLANE].reshape(N_DOM * PLANE).astype(jnp.int32)


def draw_owners(key, part):
    key = jax.random.fold_in(key, 7)

    def one_block(block_key):
        perm_key, first_key, start_key = jax.random.split(block_key, 3)
        places = jax.random.permutation(perm_key, TB).astype(jnp.int32)
        leader = jax.random.randint(first_key, (), 0, N_DOM, dtype=jnp.int32)
        back = jax.random.randint(start_key, (), 0, TB - CAP, dtype=jnp.int32)
        start = N_DOM - 2 - back
        ranks = (start + places - CAP) % (N_DOM - 1)
        others = ranks + (ranks >= leader).astype(jnp.int32)
        return jnp.where(places < CAP, leader, others)
    blocks = jax.vmap(one_block)(jax.random.split(key, N_BAND))
    return blocks.reshape(N_BAND, NT, CB).transpose(1, 0, 2).reshape(NT, NT).astype(jnp.int32)


def steps_of(stream_key, shape, shards, least, largest):
    level = 1.0
    for position, parts in shards:
        draws = jax.random.uniform(jax.random.fold_in(jax.random.fold_in(stream_key, 6), position), (parts,), jnp.float32, least / len(shards), largest / len(shards))
        level = level * jnp.repeat(jnp.exp(draws), shape[position] // parts).reshape((-1,) + (1,) * (len(shape) - 1 - position))
    return level


def centred(key, shape, spread, reach, cuts=(), held_as=jnp.bfloat16):
    factor_of = steps_of(key, shape, cuts, -0.22, 0.18) if cuts else 1.0
    values = jax.random.normal(key, shape, jnp.float32) * spread * factor_of
    return jnp.minimum(jnp.maximum(values, -reach), reach).astype(held_as)


def setup_inputs(seed: int = 0) -> dict:
    streams_of = jax.random.split(jax.random.key(seed), 9)
    return {
        "states": centred(streams_of[0], (NODES, NS), 1.0, 6.0, ((0, 64), (1, 2))),
        "mass_scale": jnp.clip(jnp.exp(math.log(2.0) - 1.3862944 * jax.random.uniform(streams_of[1], (NODES,), jnp.float32) ** steps_of(streams_of[1], (NODES,), ((0, 64),), -0.2, 0.2)), 0.5, 2.0),
        "potential": centred(streams_of[2], (QP, CELLS), 1.0, 6.0, ((1, 64),), jnp.float32),
        "kinetic": centred(streams_of[3], (NPC, NPC), NPC ** -0.5, 0.75),
        "basis_fn": centred(streams_of[4], (QP, NPC), NPC ** -0.5, 0.75),
        "connectivity": draw_connectivity(jax.random.fold_in(streams_of[8], 71), 0),
        "boundary": draw_boundary(jax.random.fold_in(streams_of[8], 71), 0),
        "owners": draw_owners(jax.random.fold_in(streams_of[8], 71), 0),
    }


CENTER = 1.0
INV_HALF = 0.25
EXACT = lax.Precision.HIGHEST


def to_half(value):
    return lax.optimization_barrier(value.astype(jnp.bfloat16)).astype(jnp.float32)


def select_slots(holder):
    count = holder.shape[0]
    spots = jnp.arange(count, dtype=jnp.int32)
    earlier = (holder[:, None] == holder[None, :]) & (spots[None, :] < spots[:, None])
    order_rank = jnp.sum(earlier.astype(jnp.int32), axis=1)
    domains = jnp.arange(N_DOM, dtype=jnp.int32)
    slots = jnp.arange(CAP, dtype=jnp.int32)
    chosen = (holder[None, None, :] == domains[:, None, None]) & (order_rank[None, None, :] == slots[None, :, None])
    return chosen.astype(jnp.float32)


def reference(states, mass_scale, potential, kinetic, basis_fn, connectivity, boundary, owners):
    state_count = states.shape[1]
    bound_list = boundary.reshape(N_DOM, PLANE)
    cell_conn = connectivity.reshape(NPC, N_DOM, CELLS_DEV).transpose(1, 0, 2)
    cell_pot = potential.reshape(QP, N_DOM, CELLS_DEV).transpose(1, 0, 2)
    kin_mat = kinetic.astype(jnp.float32)
    shape_mat = basis_fn.astype(jnp.float32)
    mass_col = mass_scale[:, None]

    def operate(values):
        scaled = to_half(mass_col * values).reshape(N_DOM, NODE_DEV, state_count)
        sent_vals = jax.vmap(lambda s, b: s[b])(scaled, bound_list)
        ghost_vals = jnp.concatenate([sent_vals[1:], jnp.zeros_like(sent_vals[:1])], 0)
        extended = jnp.concatenate([scaled, ghost_vals], 1)

        def one_domain(packed):
            ext_dev, conn_dev, pot_dev = packed
            cell_vals = ext_dev[conn_dev]
            at_points = jnp.einsum('qn,ncs->qcs', shape_mat, cell_vals, precision=EXACT)
            weighted = to_half(pot_dev[:, :, None] * at_points)
            result = jnp.einsum('qn,qcs->ncs', shape_mat, weighted, precision=EXACT)
            result = result + jnp.einsum('nm,mcs->ncs', kin_mat, cell_vals, precision=EXACT)
            return jnp.zeros((NODE_DEV + PLANE, state_count), jnp.float32).at[conn_dev].add(result)

        totals = lax.map(one_domain, (extended, cell_conn, cell_pot))
        outgoing = to_half(totals[:, NODE_DEV:])
        incoming = jnp.concatenate([jnp.zeros_like(outgoing[:1]), outgoing[:-1]], 0)
        owned = jax.vmap(lambda a, b, g: a.at[b].add(g))(totals[:, :NODE_DEV], bound_list, incoming)
        return mass_col * owned.reshape(NODES, state_count)

    start_vals = states.astype(jnp.float32)
    filtered_one = to_half((operate(start_vals) - CENTER * start_vals) * INV_HALF)
    second = to_half(2.0 * INV_HALF * (operate(filtered_one) - CENTER * filtered_one) - start_vals)
    image_vals = to_half(operate(second))
    inverse = 1.0 / NODES
    ham_proj = jnp.dot(second.T, image_vals, precision=EXACT) * inverse
    intersection_proj = jnp.dot(second.T, second, precision=EXACT) * inverse
    pair_mats = jnp.stack([ham_proj, intersection_proj])
    tile_vals = pair_mats.reshape(2, NT, TILE, NT, TILE).transpose(1, 3, 0, 2, 4).reshape(NT, NT, 2, TILE * TILE)
    results = []
    for column in range(N_BAND):
        blk_tiles = tile_vals[:, column * CB:(column + 1) * CB].reshape(TB, 2, TILE * TILE)
        holder = owners[:, column * CB:(column + 1) * CB].reshape(TB)
        chosen = select_slots(holder)
        results.append(jnp.einsum('dct,tkx->dckx', chosen, blk_tiles, precision=EXACT))
    projected = jnp.stack(results, 2).reshape(N_DOM * CAP, N_BAND, 2, TILE * TILE)
    return second.astype(jnp.bfloat16), projected
```

```python
import functools

import jax
import jax.numpy as jnp
from jax import lax
from jax.experimental import pallas as pl
from jax.experimental.pallas import tpu as pltpu
from jax.sharding import PartitionSpec as P

NPC = 64
QP = 64
TILE = 32
CAP = 4
CENTER = 1.0
INV_HALF = 0.25
EXACT = lax.Precision.HIGHEST

LANES = 128
ROWS = 128
GROUP = 4
BATCH = 8
STRIDE = 1024
F32 = jnp.float32
BF16 = jnp.bfloat16
VMEM = pl.BlockSpec(memory_space=pltpu.VMEM)
SMEM = pl.BlockSpec(memory_space=pltpu.SMEM)
ANY = pl.BlockSpec(memory_space=pl.ANY)


def round_up(count, unit):
    return -(-count // unit) * unit


def from_behind(value, axis, steps):
    count = lax.axis_size(axis)
    initial, last = (max(0, -steps), min(count, count - steps))
    return lax.ppermute(value, axis, [(source, source + steps) for source in range(initial, last)])


def params():
    return pltpu.CompilerParams(vmem_limit_bytes=62 << 20)


def by_rows(count, work):
    def step(i, _):
        work(pl.ds(pl.multiple_of(i * ROWS, ROWS), ROWS))
        return 0

    lax.fori_loop(0, count // ROWS, step, 0)


def by_entries(count, work):
    unroll = max(u for u in range(1, 65) if count % u == 0)

    def step(i, _):
        for j in range(unroll):
            work(i * unroll + j)
        return 0

    lax.fori_loop(0, count // unroll, step, 0)


def gather(src, lists, cells, out):
    for k, cell in enumerate(cells):
        for j in range(NPC):
            out[k * NPC + j : k * NPC + j + 1, :] = src[pl.ds(lists[j][cell], 1), :]


def multiply(vals, pot, base, stacked, basis_t, out):
    chunk = pl.multiple_of((base // LANES) * LANES, LANES)
    shift = lax.rem(LANES - lax.rem(base, LANES), LANES)
    columns = pltpu.roll(pot[:, pl.ds(chunk, LANES)], shift, 1)
    for p in range(0, GROUP, 2):
        pair = jnp.concatenate(
            [vals[k * NPC : (k + 1) * NPC, :] for k in (p, p + 1)], axis=1
        ).astype(BF16)
        both = jnp.dot(stacked, pair, preferred_element_type=F32)
        weight = jnp.concatenate(
            [jnp.broadcast_to(columns[:, k : k + 1], (QP, LANES)) for k in (p, p + 1)], axis=1
        )
        weighted = (weight * both[:QP]).astype(BF16)
        result = jnp.dot(basis_t, weighted, preferred_element_type=F32) + both[QP:]
        for k in (p, p + 1):
            out[k * NPC : (k + 1) * NPC, :] = result[:, (k - p) * LANES : (k - p + 1) * LANES]


def scatter(res, lists, cells, sums, batch):
    for p in range(0, GROUP, 2):
        for start in range(0, NPC, batch):
            moved = []
            for k in (p, p + 1):
                for j in range(start, start + batch):
                    row = pl.ds(lists[j][cells[k]], 1)
                    total = sums[k - p][row, :] + res[k * NPC + j : k * NPC + j + 1, :]
                    moved.append((k - p, row, total))
            for which, row, total in moved:
                sums[which][row, :] = total


def cells_of(group):
    return [group * GROUP + k for k in range(GROUP)]


def sweep(groups, src, lists, pot, stacked_ref, basis_t_ref, sums, vals, ress, repeated):
    stacked = stacked_ref[...]
    basis_t = basis_t_ref[...]

    def mult(slot, group):
        multiply(vals[slot], pot, group * GROUP, stacked, basis_t, ress[slot])

    def two(i, _):
        first = 2 * i
        gather(src, lists, cells_of(first + 1), vals[1])
        mult(0, first)
        scatter(ress[1], lists, cells_of(jnp.maximum(first - 1, 0)), sums, BATCH)
        gather(src, lists, cells_of(jnp.minimum(first + 2, groups - 1)), vals[0])
        mult(1, first + 1)
        scatter(ress[0], lists, cells_of(first), sums, BATCH)
        return 0

    @pl.when(repeated[0] == 0)
    def _():
        ress[1][...] = jnp.zeros_like(ress[1])
        gather(src, lists, cells_of(0), vals[0])
        lax.fori_loop(0, groups // 2, two, 0)
        scatter(ress[1], lists, cells_of(groups - 1), sums, BATCH)

    @pl.when(repeated[0] != 0)
    def _():
        def one(i, _):
            gather(src, lists, cells_of(i), vals[0])
            mult(0, i)
            scatter(ress[0], lists, cells_of(i), sums, 1)
            return 0

        lax.fori_loop(0, groups, one, 0)


def edge_kernel(edge_count, edge, states, mass, states_edge, mass_edge, wide):
    def widen(rows):
        wide[rows, :] = states[rows, :].astype(F32)

    by_rows(states.shape[0], widen)
    tail = states_edge.shape[0] - 8
    states_edge[tail:, :] = jnp.zeros((8, LANES), F32)
    mass_edge[tail:, :] = jnp.zeros((8, LANES), F32)

    def take(i):
        row = pl.ds(edge[i], 1)
        states_edge[pl.ds(i, 1), :] = wide[row, :]
        mass_edge[pl.ds(i, 1), :] = mass[row, :]

    by_entries(edge_count, take)


def apply_kernel(which, sizes, *refs):
    nodes, padded, edge_count, groups = sizes
    refs = list(refs)
    conn, edge, repeated, pot, stacked, basis_t, mass, values, ghost = refs[:9]
    del refs[:9]
    if which > 1:
        scaled_edge = refs.pop(0)
    if which == 2:
        states = refs.pop(0)
    if which == 3:
        second_edge = refs.pop(0)
    result, edge_sums, outgoing = refs[:3]
    del refs[:3]
    if which == 3:
        second = refs.pop(0)
    src, sum_a, sum_b, val_a, val_b, res_a, res_b, arrived = refs[:8]
    lists = refs[8:]
    copies = [
        pltpu.make_async_copy(conn.at[pl.ds(j * STRIDE, STRIDE)], lists[j], arrived.at[j])
        for j in range(NPC)
    ]
    for copy in copies:
        copy.start()
    ghost_count = ghost.shape[0]

    def prepare(rows):
        scaled = (mass[rows, :] * values[rows, :].astype(F32)).astype(BF16)
        src[rows, :] = scaled.astype(F32)

    by_rows(padded, prepare)
    src[padded : padded + ghost_count, :] = ghost[...].astype(F32)
    if which > 1:

        def patch(i):
            src[pl.ds(edge[i], 1), :] = scaled_edge[pl.ds(i, 1), :]

        by_entries(edge_count, patch)

    def clear(rows):
        sum_a[rows, :] = jnp.zeros((ROWS, LANES), F32)
        sum_b[rows, :] = jnp.zeros((ROWS, LANES), F32)

    by_rows(src.shape[0], clear)
    for copy in copies:
        copy.wait()

    sweep(
        groups,
        src,
        lists,
        pot,
        stacked,
        basis_t,
        (sum_a, sum_b),
        (val_a, val_b),
        (res_a, res_b),
        repeated,
    )

    ghost_rows = slice(padded, padded + ghost_count)
    outgoing[...] = (sum_a[ghost_rows, :] + sum_b[ghost_rows, :]).astype(BF16)
    tail = edge_sums.shape[0] - 8
    edge_sums[tail:, :] = jnp.zeros((8, LANES), F32)

    def take(i):
        row = pl.ds(edge[i], 1)
        edge_sums[pl.ds(i, 1), :] = sum_a[row, :] + sum_b[row, :]
        if which == 3:
            sum_a[row, :] = jnp.zeros((1, LANES), F32)
            sum_b[row, :] = jnp.zeros((1, LANES), F32)

    by_entries(edge_count, take)

    def finish(rows):
        image = mass[rows, :] * (sum_a[rows, :] + sum_b[rows, :])
        if which == 1:
            result[rows, :] = ((image - CENTER * values[rows, :].astype(F32)) * INV_HALF).astype(BF16)
        elif which == 2:
            result[rows, :] = (
                2.0 * INV_HALF * (image - CENTER * values[rows, :].astype(F32))
                - states[rows, :].astype(F32)
            ).astype(BF16)
        else:
            result[rows, :LANES] = image.astype(BF16)
            src[rows, :] = values[rows, :].astype(F32)

    by_rows(padded, finish)
    if which == 3:

        def blank(i):
            src[pl.ds(edge[i], 1), :] = jnp.zeros((1, LANES), F32)

        def fill(i):
            src[pl.ds(edge[i], 1), :] = second_edge[pl.ds(i, 1), :]

        def blanked(rows):
            result[rows, LANES:] = src[rows, :].astype(BF16)

        def filled(rows):
            second[rows, :] = src[rows, :].astype(BF16)

        by_entries(edge_count, blank)
        by_rows(padded, blanked)
        by_entries(edge_count, fill)
        whole = nodes // ROWS * ROWS
        by_rows(whole, filled)
        second[whole:nodes, :] = src[whole:nodes, :].astype(BF16)


def local(states, mass_scale, potential, kinetic, basis_fn, connectivity, boundary, owners):
    node_count, state_count = states.shape
    edge_count = boundary.shape[0]
    cell_count = connectivity.shape[1]
    padded = round_up(node_count, ROWS)
    edge_rows = round_up(edge_count, 16)
    total_rows = round_up(padded + edge_rows, ROWS)

    is_ghost = connectivity >= node_count
    lists = jnp.where(is_ghost, connectivity + (padded - node_count), connectivity)
    lists = jnp.pad(lists, ((0, 0), (0, STRIDE - cell_count))).reshape(-1)
    batched = jnp.where(is_ghost, connectivity, -1).reshape(NPC // BATCH, BATCH, cell_count)
    same = (batched[:, :, None] == batched[:, None, :]) & (batched[:, :, None] >= 0)
    apart = ~jnp.eye(BATCH, dtype=bool)[None, :, :, None]
    repeated = jnp.any(same & apart).astype(jnp.int32).reshape(1)
    pot = jnp.pad(potential, ((0, 0), (0, round_up(cell_count, LANES) - cell_count)))
    mass = jnp.pad(
        jnp.broadcast_to(mass_scale[:, None], (node_count, LANES)),
        ((0, padded - node_count), (0, 0)),
    )
    states_padded = jnp.pad(states, ((0, padded - node_count), (0, 0)))
    stacked = jnp.concatenate([basis_fn, kinetic], 0)
    basis_t = basis_fn.T

    edge_shape = jax.ShapeDtypeStruct((edge_rows, LANES), F32)
    edge_half = jax.ShapeDtypeStruct((edge_rows, LANES), BF16)
    wide_half = jax.ShapeDtypeStruct((padded, LANES), BF16)
    both_half = jax.ShapeDtypeStruct((padded, 2 * LANES), BF16)
    states_edge, mass_edge = pl.pallas_call(
        functools.partial(edge_kernel, edge_count),
        out_shape=(edge_shape, edge_shape),
        in_specs=[SMEM, VMEM, VMEM],
        out_specs=(VMEM, VMEM),
        scratch_shapes=[pltpu.VMEM((padded, LANES), F32)],
        compiler_params=params(),
        name="edge_rows",
    )(boundary, states_padded, mass)

    work = pltpu.VMEM((total_rows, LANES), F32)
    block = pltpu.VMEM((GROUP * NPC, LANES), F32)

    def operate(which, values, ghost, extra, outs):
        sizes = (node_count, padded, edge_count, cell_count // GROUP)
        return pl.pallas_call(
            functools.partial(apply_kernel, which, sizes),
            out_shape=outs,
            in_specs=[ANY, SMEM, SMEM] + [VMEM] * (6 + len(extra)),
            out_specs=(VMEM,) * len(outs),
            scratch_shapes=[work, work, work, block, block, block, block]
            + [pltpu.SemaphoreType.DMA((NPC,))]
            + [pltpu.SMEM((STRIDE,), jnp.int32)] * NPC,
            compiler_params=params(),
            name=f"apply_{which}",
        )(lists, boundary, repeated, pot, stacked, basis_t, mass, values, ghost, *extra)

    def joined(edge_sums, outgoing):
        incoming = from_behind(outgoing, "dom", 1)
        return mass_edge * (edge_sums + incoming.astype(F32))

    def scaled(edge):
        return (mass_edge * edge).astype(BF16)

    sent = scaled(states_edge)
    ghost = from_behind(sent, "dom", -1)
    one, sums, outgoing = operate(1, states_padded, ghost, (), (wide_half, edge_shape, edge_half))
    one_edge = ((joined(sums, outgoing) - CENTER * states_edge) * INV_HALF).astype(BF16).astype(F32)

    sent = scaled(one_edge)
    ghost = from_behind(sent, "dom", -1)
    two, sums, outgoing = operate(
        2, one, ghost, (sent.astype(F32), states_padded), (wide_half, edge_shape, edge_half)
    )
    shard_cols = lax.all_gather(two, "band", axis=1, tiled=True)
    two_half = (
        2.0 * INV_HALF * (joined(sums, outgoing) - CENTER * one_edge) - states_edge
    ).astype(BF16)
    two_edge = two_half.astype(F32)

    sent = scaled(two_edge)
    ghost = from_behind(sent, "dom", -1)
    edge_cols = lax.all_gather(two_half, "band", axis=1, tiled=True)
    own, sums, outgoing, second = operate(
        3,
        two,
        ghost,
        (sent.astype(F32), two_edge),
        (both_half, edge_shape, edge_half, jax.ShapeDtypeStruct((node_count, LANES), BF16)),
    )
    image_edge = joined(sums, outgoing).astype(BF16)
    own_edge = jnp.concatenate([image_edge, two_half], 1)

    def project(columns, mine):
        return lax.dot_general(
            columns, mine, (((0,), (0,)), ((), ())), preferred_element_type=F32
        )

    pair = project(shard_cols, own) + project(edge_cols, own_edge)
    inverse = 1.0 / (node_count * lax.axis_size("dom"))
    pair = lax.psum(pair * inverse, "dom")

    tile_rows = pair.shape[0] // TILE
    tile_cols = state_count // TILE
    tile_count = tile_rows * tile_cols
    tile_vals = (
        pair.reshape(tile_rows, TILE, 2, tile_cols, TILE)
        .transpose(0, 3, 2, 1, 4)
        .reshape(tile_count, 2 * TILE * TILE)
    )
    holder = lax.dynamic_slice_in_dim(
        owners, lax.axis_index("band") * tile_cols, tile_cols, 1
    ).reshape(tile_count)
    spots = jnp.arange(tile_count, dtype=jnp.int32)
    earlier = (holder[:, None] == holder[None, :]) & (spots[None, :] < spots[:, None])
    order_rank = jnp.sum(earlier.astype(jnp.int32), axis=1)
    slots = jnp.arange(CAP, dtype=jnp.int32)
    chosen = (holder[None, :] == lax.axis_index("dom")) & (order_rank[None, :] == slots[:, None])
    mine = jnp.dot(chosen.astype(F32), tile_vals, precision=EXACT)
    return (second, mine.reshape(CAP, 1, 2, TILE * TILE))


def solution(mesh):
    return jax.shard_map(
        local,
        mesh=mesh,
        in_specs=(
            P("dom", "band"),
            P("dom"),
            P(None, "dom"),
            P(),
            P(),
            P(None, "dom"),
            P("dom"),
            P(),
        ),
        out_specs=(P("dom", "band"), P("dom", "band", None, None)),
        check_vma=False,
    )
```

```python
import functools

import jax
import jax.numpy as jnp
from jax import lax
from jax.experimental import pallas as pl
from jax.experimental.pallas import tpu as pltpu
from jax.sharding import PartitionSpec as P

NPC = 64
QP = 64
TILE = 32
CAP = 4
CENTER = 1.0
INV_HALF = 0.25
EXACT = lax.Precision.HIGHEST
DIMS = (2, 4, 4, 2)

LANES = 128
ROWS = 128
GROUP = 4
TURN = 2 * GROUP
BATCH = 8
SCOPED = 30
STRIDE = 1024
F32 = jnp.float32
BF16 = jnp.bfloat16
VMEM = pl.BlockSpec(memory_space=pltpu.VMEM)
SMEM = pl.BlockSpec(memory_space=pltpu.SMEM)
ANY = pl.BlockSpec(memory_space=pl.ANY)


def round_up(count, unit):
    return -(-count // unit) * unit


def from_behind(value, axis, steps):
    count = lax.axis_size(axis)
    initial, last = (max(0, -steps), min(count, count - steps))
    return lax.ppermute(value, axis, [(source, source + steps) for source in range(initial, last)])


def params(mebibytes):
    return pltpu.CompilerParams(vmem_limit_bytes=mebibytes << 20)


def cost(us):
    return pl.CostEstimate(flops=us * 10**9, bytes_accessed=us * 10**6, transcendentals=0)


def by_rows(count, work):
    def step(i, _):
        work(pl.ds(pl.multiple_of(i * ROWS, ROWS), ROWS))
        return 0

    lax.fori_loop(0, count // ROWS, step, 0)


def by_entries(count, work):
    unroll = max(u for u in range(1, 65) if count % u == 0)

    def step(i, _):
        for j in range(unroll):
            work(i * unroll + j)
        return 0

    lax.fori_loop(0, count // unroll, step, 0)


def gather(src, lists, cells, out):
    for k, cell in enumerate(cells):
        for j in range(NPC):
            out[k * NPC + j : k * NPC + j + 1, :] = src[pl.ds(lists[j][cell], 1), :]


def multiply(vals, pot, base, stacked, basis_t, out):
    chunk = pl.multiple_of((base // LANES) * LANES, LANES)
    shift = lax.rem(LANES - lax.rem(base, LANES), LANES)
    columns = pltpu.roll(pot[:, pl.ds(chunk, LANES)], shift, 1)
    for p in range(0, GROUP, 2):
        pair = jnp.concatenate(
            [vals[k * NPC : (k + 1) * NPC, :] for k in (p, p + 1)], axis=1
        ).astype(BF16)
        both = jnp.dot(stacked, pair, preferred_element_type=F32)
        weight = jnp.concatenate(
            [jnp.broadcast_to(columns[:, k : k + 1], (QP, LANES)) for k in (p, p + 1)], axis=1
        )
        weighted = (weight * both[:QP]).astype(BF16)
        result = jnp.dot(basis_t, weighted, preferred_element_type=F32) + both[QP:]
        for k in (p, p + 1):
            out[k * NPC : (k + 1) * NPC, :] = result[:, (k - p) * LANES : (k - p + 1) * LANES]


def scatter(res, lists, cells, sums, batch):
    for p in range(0, GROUP, 2):
        for start in range(0, NPC, batch):
            moved = []
            for k in (p, p + 1):
                for j in range(start, start + batch):
                    row = pl.ds(lists[j][cells[k]], 1)
                    total = sums[k - p][row, :] + res[k * NPC + j : k * NPC + j + 1, :]
                    moved.append((k - p, row, total))
            for which, row, total in moved:
                sums[which][row, :] = total


def cells_of(group):
    return [group * GROUP + k for k in range(GROUP)]


def sweep(begin, end, repeated, src, lists, pot, stacked_ref, basis_t_ref, sums, vals, ress):
    def mult(slot, group, stacked, basis_t):
        multiply(vals[slot], pot, group * GROUP, stacked, basis_t, ress[slot])

    def two(i, _):
        stacked, basis_t = stacked_ref[...], basis_t_ref[...]
        first = 2 * i
        gather(src, lists, cells_of(first + 1), vals[1])
        mult(0, first, stacked, basis_t)
        scatter(ress[1], lists, cells_of(jnp.maximum(first - 1, 2 * begin)), sums, BATCH)
        gather(src, lists, cells_of(jnp.minimum(first + 2, 2 * end - 1)), vals[0])
        mult(1, first + 1, stacked, basis_t)
        scatter(ress[0], lists, cells_of(first), sums, BATCH)
        return 0

    @pl.when((end > begin) & (repeated == 0))
    def _():
        ress[1][...] = jnp.zeros_like(ress[1])
        gather(src, lists, cells_of(2 * begin), vals[0])
        lax.fori_loop(begin, end, two, 0)
        scatter(ress[1], lists, cells_of(2 * end - 1), sums, BATCH)

    @pl.when((end > begin) & (repeated != 0))
    def _():
        def one(i, _):
            gather(src, lists, cells_of(i), vals[0])
            mult(0, i, stacked_ref[...], basis_t_ref[...])
            scatter(ress[0], lists, cells_of(i), sums, 1)
            return 0

        lax.fori_loop(2 * begin, 2 * end, one, 0)


def start_kernel(
    edge_count, edge, states, mass_rows, mass, kept, src, sum_a, sum_b, states_edge, mass_edge, sent
):
    nodes = states.shape[0]
    padded = kept.shape[0]
    whole = nodes // ROWS * ROWS

    def widen(rows):
        sum_a[rows, :] = states[rows, :].astype(F32)

    by_rows(whole, widen)
    if whole < padded:
        sum_a[whole:padded, :] = jnp.zeros((padded - whole, LANES), F32)
        sum_a[whole:nodes, :] = states[whole:nodes, :].astype(F32)

    def scale(i, _):
        rows = pl.ds(pl.multiple_of(i * ROWS, ROWS), ROWS)
        column = jnp.broadcast_to(mass_rows[pl.ds(i, 1), :], (ROWS, LANES)).T
        value = sum_a[rows, :]
        mass[rows, :] = column
        kept[rows, :] = value.astype(BF16)
        src[rows, :] = (column * value).astype(BF16).astype(F32)
        return 0

    lax.fori_loop(0, padded // ROWS, scale, 0)
    tail = states_edge.shape[0] - 8
    states_edge[tail:, :] = jnp.zeros((8, LANES), F32)
    mass_edge[tail:, :] = jnp.zeros((8, LANES), F32)

    def take(i):
        row = pl.ds(edge[i], 1)
        states_edge[pl.ds(i, 1), :] = sum_a[row, :]
        mass_edge[pl.ds(i, 1), :] = mass[row, :]

    by_entries(edge_count, take)
    sent[...] = (mass_edge[...] * states_edge[...]).astype(BF16)
    src[padded:, :] = jnp.zeros((src.shape[0] - padded, LANES), F32)

    def clear(rows):
        sum_a[rows, :] = jnp.zeros((ROWS, LANES), F32)
        sum_b[rows, :] = jnp.zeros((ROWS, LANES), F32)

    by_rows(sum_a.shape[0], clear)


def cells_kernel(part, which, edge_count, padded, *refs):
    refs = list(refs)
    conn, counts, pot, stacked, basis_t, src, sum_a, sum_b = refs[:8]
    refs = refs[8:]
    if part == 0 and which > 1:
        edge, scaled_edge = refs[:2]
        refs = refs[2:]
    if part == 1:
        ghost = refs.pop(0)
    sources = []
    if part == 2:
        edge = refs.pop(0)
        if which == 3:
            second_edge = refs.pop(0)
        loads = 3 if which == 2 else 2
        sources, refs = refs[:loads], refs[loads:]
    refs = refs[3:]
    if part == 1:
        outgoing = refs.pop(0)
    if part == 2:
        edge_sums, result = refs[:2]
        refs = refs[2:]
        if which == 3:
            second = refs.pop(0)
    val_a, val_b, res_a, res_b, arrived = refs[:5]
    lists, refs = refs[5 : 5 + NPC], refs[5 + NPC :]
    if part == 2:
        loaded, refs = refs[0], refs[1:]
        fetches = [
            pltpu.make_async_copy(source, ref, loaded.at[n])
            for n, (source, ref) in enumerate(zip(sources, refs))
        ]
    copies = [
        pltpu.make_async_copy(conn.at[pl.ds(j * STRIDE, STRIDE)], lists[j], arrived.at[j])
        for j in range(NPC)
    ]
    for copy in copies:
        copy.start()
    if part == 2:
        for fetch in fetches:
            fetch.start()
    if part == 0 and which > 1:

        def patch(i):
            src[pl.ds(edge[i], 1), :] = scaled_edge[pl.ds(i, 1), :]

        by_entries(edge_count, patch)
    if part == 1:
        src[padded : padded + ghost.shape[0], :] = ghost[...].astype(F32)
    for copy in copies:
        copy.wait()

    begin, end = ((0, counts[0]), (counts[1], counts[2]), (counts[0], counts[1]))[part]
    sums = (sum_a, sum_b)
    sweep(
        begin,
        end,
        counts[3],
        src,
        lists,
        pot,
        stacked,
        basis_t,
        sums,
        (val_a, val_b),
        (res_a, res_b),
    )
    if part == 1:
        ghost_rows = slice(padded, padded + ghost.shape[0])
        outgoing[...] = (sum_a[ghost_rows, :] + sum_b[ghost_rows, :]).astype(BF16)
        blank = jnp.zeros(ghost.shape, F32)
        sum_a[ghost_rows, :] = blank
        sum_b[ghost_rows, :] = blank
    if part < 2:
        return

    for fetch in fetches:
        fetch.wait()
    mass, values = refs[:2]
    tail = edge_sums.shape[0] - 8
    edge_sums[tail:, :] = jnp.zeros((8, LANES), F32)

    def take(i):
        row = pl.ds(edge[i], 1)
        edge_sums[pl.ds(i, 1), :] = sum_a[row, :] + sum_b[row, :]
        if which == 3:
            sum_a[row, :] = jnp.zeros((1, LANES), F32)
            sum_b[row, :] = jnp.zeros((1, LANES), F32)

    by_entries(edge_count, take)

    def finish(rows):
        scale = mass[rows, :]
        image = scale * (sum_a[rows, :] + sum_b[rows, :])
        value = values[rows, :].astype(F32)
        if which == 3:
            result[rows, :LANES] = image.astype(BF16)
            src[rows, :] = value
            return
        if which == 1:
            after = ((image - CENTER * value) * INV_HALF).astype(BF16)
        else:
            start = refs[2][rows, :].astype(F32)
            after = (2.0 * INV_HALF * (image - CENTER * value) - start).astype(BF16)
        result[rows, :] = after
        src[rows, :] = (scale * after.astype(F32)).astype(BF16).astype(F32)
        sum_a[rows, :] = jnp.zeros((ROWS, LANES), F32)
        sum_b[rows, :] = jnp.zeros((ROWS, LANES), F32)

    by_rows(padded, finish)
    if which == 3:

        def blank(i):
            src[pl.ds(edge[i], 1), :] = jnp.zeros((1, LANES), F32)

        def fill(i):
            src[pl.ds(edge[i], 1), :] = second_edge[pl.ds(i, 1), :]

        def blanked(rows):
            result[rows, LANES:] = src[rows, :].astype(BF16)

        def filled(rows):
            second[rows, :] = src[rows, :].astype(BF16)

        nodes = second.shape[0]
        by_entries(edge_count, blank)
        by_rows(padded, blanked)
        by_entries(edge_count, fill)
        whole = nodes // ROWS * ROWS
        by_rows(whole, filled)
        if whole < nodes:
            second[whole:nodes, :] = src[whole:nodes, :].astype(BF16)


def arrange(connectivity, potential, node_count, padded):
    cell_count = connectivity.shape[1]
    is_ghost = connectivity >= node_count
    late = jnp.any(is_ghost, axis=0).astype(F32)[None]
    before = jnp.triu(jnp.ones((cell_count, cell_count), F32), 1)
    ranks = jnp.dot(jnp.concatenate([late, 1.0 - late], 0), before, precision=EXACT)
    late_count = jnp.sum(late).astype(jnp.int32)
    turns = (cell_count - late_count + TURN - 1) // TURN
    late_turns = (late_count + TURN - 1) // TURN
    place = jnp.where(late[0] > 0, (turns * TURN).astype(F32) + ranks[0], ranks[1])
    slots = round_up(round_up(cell_count, TURN) + TURN, LANES)
    hot = (place[:, None] == jnp.arange(slots, dtype=F32)[None, :]).astype(F32)
    moved = jnp.dot(
        jnp.concatenate([connectivity.astype(F32), potential], 0), hot, precision=EXACT
    )
    index = jnp.round(moved[:NPC]).astype(jnp.int32)
    index = jnp.where(index >= node_count, index + (padded - node_count), index)
    used = jnp.sum(hot, axis=0) > 0
    spare = node_count + jnp.arange(NPC, dtype=jnp.int32)
    index = jnp.where(used[None, :], index, spare[:, None])
    lists = jnp.pad(index, ((0, 0), (0, STRIDE - slots))).reshape(-1)

    batched = jnp.where(is_ghost, connectivity, -1).reshape(NPC // BATCH, BATCH, cell_count)
    same = (batched[:, :, None] == batched[:, None, :]) & (batched[:, :, None] >= 0)
    apart = ~jnp.eye(BATCH, dtype=bool)[None, :, :, None]
    repeated = jnp.any(same & apart).astype(jnp.int32)
    counts = jnp.stack([turns // 2, turns, turns + late_turns, repeated])
    return lists, moved[NPC:], counts


def swap(value, dim, offset):
    step = 1
    for size in DIMS[dim + 1 :]:
        step *= size
    count, total = DIMS[dim], lax.axis_size("dom")
    pairs = []
    for source in range(total):
        digit = source // step % count
        pairs.append((source, source + ((digit + offset) % count - digit) * step))
    return lax.ppermute(value, "dom", pairs)


def to_owners(tiles, holder):
    here = lax.axis_index("dom")

    def digits(index):
        found = []
        for size in reversed(DIMS):
            found.append(index % size)
            index = index // size
        return found[::-1]

    mine, owner = digits(here), digits(holder)
    count = holder.shape[0]
    before = jnp.arange(count)[:, None] < jnp.arange(count)[None, :]

    def chosen(member, slots):
        rank = jnp.sum((member[:, None] & before).astype(jnp.int32), axis=0)
        return (member[None, :] & (rank[None, :] == jnp.arange(slots)[:, None])).astype(F32)

    column = (owner[0] == mine[0]) & (owner[3] == mine[3])
    plane_slots = min(count, DIMS[1] * CAP)
    for_plane = [
        chosen(column & (owner[2] == (mine[2] + k) % DIMS[2]), plane_slots)
        for k in range(DIMS[2])
    ]
    for_row = [
        chosen(column & (owner[2] == mine[2]) & (owner[1] == (mine[1] + k) % DIMS[1]), CAP)
        for k in range(DIMS[1])
    ]
    by_row = jnp.einsum("kst,ut->ksu", jnp.stack(for_row), for_plane[0], precision=EXACT)
    tiles = tiles + swap(tiles, 3, 1)
    tiles = tiles + swap(tiles, 0, 1)
    parts = jnp.dot(jnp.concatenate(for_plane, 0), tiles, precision=EXACT)
    parts = parts.reshape(DIMS[2], plane_slots, tiles.shape[1])
    total = parts[0]
    for arrived in [swap(parts[k], 2, k) for k in range(1, DIMS[2])]:
        total = total + arrived
    parts = jnp.dot(by_row.reshape(DIMS[1] * CAP, plane_slots), total, precision=EXACT)
    parts = parts.reshape(DIMS[1], CAP, tiles.shape[1])
    total = parts[0]
    for arrived in [swap(parts[k], 1, k) for k in range(1, DIMS[1])]:
        total = total + arrived
    return total


def local(states, mass_scale, potential, kinetic, basis_fn, connectivity, boundary, owners):
    node_count, state_count = states.shape
    edge_count = boundary.shape[0]
    padded = round_up(node_count + NPC, ROWS)
    edge_rows = round_up(edge_count + 7, 16)
    total_rows = round_up(padded + edge_rows, ROWS)

    wide = pltpu.VMEM((total_rows, LANES), F32)
    edge_shape = jax.ShapeDtypeStruct((edge_rows, LANES), F32)
    edge_half = jax.ShapeDtypeStruct((edge_rows, LANES), BF16)
    padded_half = jax.ShapeDtypeStruct((padded, LANES), BF16)
    both_half = jax.ShapeDtypeStruct((padded, 2 * LANES), BF16)
    whole_half = jax.ShapeDtypeStruct((node_count, LANES), BF16)

    mass_rows = jnp.pad(mass_scale, (0, padded - node_count)).reshape(padded // ROWS, ROWS)
    mass, kept, src, sum_a, sum_b, states_edge, mass_edge, sent = pl.pallas_call(
        functools.partial(start_kernel, edge_count),
        out_shape=(jax.ShapeDtypeStruct((padded, LANES), F32), padded_half, wide, wide, wide)
        + (edge_shape, edge_shape, edge_half),
        in_specs=[SMEM, VMEM, VMEM],
        out_specs=(VMEM,) * 8,
        compiler_params=params(SCOPED),
        cost_estimate=cost(10),
        name="start",
    )(boundary, states, mass_rows)
    ghost = from_behind(sent, "dom", -1)
    lists, pot, counts = arrange(connectivity, potential, node_count, padded)
    stacked = jnp.concatenate([basis_fn, kinetic], 0)
    basis_t = basis_fn.T
    block = pltpu.VMEM((GROUP * NPC, LANES), F32)

    def cells(part, which, held, specs, extra, outs, scratch=()):
        return pl.pallas_call(
            functools.partial(cells_kernel, part, which, edge_count, padded),
            out_shape=(wide, wide, wide) + outs,
            in_specs=[ANY, SMEM] + [VMEM] * 6 + specs,
            out_specs=(VMEM,) * (3 + len(outs)),
            input_output_aliases={5: 0, 6: 1, 7: 2},
            scratch_shapes=[block, block, block, block]
            + [pltpu.SemaphoreType.DMA((NPC,))]
            + [pltpu.SMEM((STRIDE,), jnp.int32)] * NPC
            + list(scratch),
            compiler_params=params(SCOPED),
            cost_estimate=cost(20),
            name=f"cells_{which}_{part}",
        )(lists, counts, pot, stacked, basis_t, *held, *extra)

    def joined(edge_sums, outgoing):
        incoming = from_behind(outgoing, "dom", 1)
        return mass_edge * (edge_sums + incoming.astype(F32))

    def scaled(edge):
        return (mass_edge * edge).astype(BF16)

    loaded = pltpu.SemaphoreType.DMA((3,))
    mass_room = pltpu.VMEM((padded, LANES), F32)
    half_room = pltpu.VMEM((padded, LANES), BF16)
    held = cells(0, 1, (src, sum_a, sum_b), [], (), ())
    *held, outgoing = cells(1, 1, held, [VMEM], (ghost,), (edge_half,))
    *held, sums, one = cells(
        2,
        1,
        held,
        [SMEM, ANY, ANY],
        (boundary, mass, kept),
        (edge_shape, padded_half),
        (loaded, mass_room, half_room),
    )
    one_edge = ((joined(sums, outgoing) - CENTER * states_edge) * INV_HALF).astype(BF16).astype(F32)

    sent = scaled(one_edge)
    ghost = from_behind(sent, "dom", -1)
    held = cells(0, 2, held, [SMEM, VMEM], (boundary, sent.astype(F32)), ())
    *held, outgoing = cells(1, 2, held, [VMEM], (ghost,), (edge_half,))
    *held, sums, two = cells(
        2,
        2,
        held,
        [SMEM, ANY, ANY, ANY],
        (boundary, mass, one, kept),
        (edge_shape, padded_half),
        (loaded, mass_room, half_room, half_room),
    )
    turned = [(0, 1), (1, 0)]
    other = lax.ppermute(two, "band", turned)
    two_half = (
        2.0 * INV_HALF * (joined(sums, outgoing) - CENTER * one_edge) - states_edge
    ).astype(BF16)
    two_edge = two_half.astype(F32)
    other_edge = lax.ppermute(two_half, "band", turned)

    sent = scaled(two_edge)
    ghost = from_behind(sent, "dom", -1)
    held = cells(0, 3, held, [SMEM, VMEM], (boundary, sent.astype(F32)), ())
    *held, outgoing = cells(1, 3, held, [VMEM], (ghost,), (edge_half,))
    *held, sums, own, second = cells(
        2,
        3,
        held,
        [SMEM, VMEM, ANY, ANY],
        (boundary, two_edge, mass, two),
        (edge_shape, both_half, whole_half),
        (loaded, mass_room, half_room),
    )
    image_edge = joined(sums, outgoing).astype(BF16)
    own_edge = jnp.concatenate([image_edge, two_half], 1)

    def project(columns, mine):
        return lax.dot_general(
            columns, mine, (((0,), (0,)), ((), ())), preferred_element_type=F32
        )

    inverse = 1.0 / (node_count * lax.axis_size("dom"))
    near = (project(two, own) + project(two_half, own_edge)) * inverse
    far = (project(other, own) + project(other_edge, own_edge)) * inverse
    lower = lax.axis_index("band") == 0
    pair = jnp.concatenate([jnp.where(lower, near, far), jnp.where(lower, far, near)], 0)

    tile_rows = pair.shape[0] // TILE
    tile_cols = state_count // TILE
    tile_count = tile_rows * tile_cols
    tile_vals = (
        pair.reshape(tile_rows, TILE, 2, tile_cols, TILE)
        .transpose(0, 3, 2, 1, 4)
        .reshape(tile_count, 2 * TILE * TILE)
    )
    holder = lax.dynamic_slice_in_dim(
        owners, lax.axis_index("band") * tile_cols, tile_cols, 1
    ).reshape(tile_count)
    mine = to_owners(tile_vals, holder)
    return (second, mine.reshape(CAP, 1, 2, TILE * TILE))


def solution(mesh):
    return jax.shard_map(
        local,
        mesh=mesh,
        in_specs=(
            P("dom", "band"),
            P("dom"),
            P(None, "dom"),
            P(),
            P(),
            P(None, "dom"),
            P("dom"),
            P(),
        ),
        out_specs=(P("dom", "band"), P("dom", "band", None, None)),
        check_vma=False,
    )
```

```python
import functools

import jax
import jax.numpy as jnp
from jax import lax
from jax.experimental import pallas as pl
from jax.experimental.pallas import tpu as pltpu
from jax.sharding import PartitionSpec as P

NPC = 64
QP = 64
TILE = 32
CAP = 4
CENTER = 1.0
INV_HALF = 0.25
EXACT = lax.Precision.HIGHEST
DIMS = (2, 4, 4, 2)

LANES = 128
ROWS = 128
GROUP = 4
TURN = 2 * GROUP
BATCH = 8
SCOPED = 24
STRIDE = 1024
F32 = jnp.float32
BF16 = jnp.bfloat16
VMEM = pl.BlockSpec(memory_space=pltpu.VMEM)
SMEM = pl.BlockSpec(memory_space=pltpu.SMEM)
ANY = pl.BlockSpec(memory_space=pl.ANY)


def round_up(count, unit):
    return -(-count // unit) * unit


def from_behind(value, axis, steps):
    count = lax.axis_size(axis)
    initial, last = (max(0, -steps), min(count, count - steps))
    return lax.ppermute(value, axis, [(source, source + steps) for source in range(initial, last)])


def params(mebibytes):
    return pltpu.CompilerParams(vmem_limit_bytes=mebibytes << 20)


def cost(us):
    return pl.CostEstimate(flops=us * 10**9, bytes_accessed=us * 10**6, transcendentals=0)


def by_rows(count, work):
    def step(i, _):
        work(pl.ds(pl.multiple_of(i * ROWS, ROWS), ROWS))
        return 0

    lax.fori_loop(0, count // ROWS, step, 0)


def by_entries(count, work):
    unroll = max(u for u in range(1, 65) if count % u == 0)

    def step(i, _):
        for j in range(unroll):
            work(i * unroll + j)
        return 0

    lax.fori_loop(0, count // unroll, step, 0)


def gather(src, lists, cells, out):
    for k, cell in enumerate(cells):
        for j in range(NPC):
            out[k * NPC + j : k * NPC + j + 1, :] = src[pl.ds(lists[j][cell], 1), :]


def multiply(vals, pot, base, stacked, basis_t, out):
    chunk = pl.multiple_of((base // LANES) * LANES, LANES)
    shift = lax.rem(LANES - lax.rem(base, LANES), LANES)
    columns = pltpu.roll(pot[:, pl.ds(chunk, LANES)], shift, 1)
    for p in range(0, GROUP, 2):
        pair = jnp.concatenate(
            [vals[k * NPC : (k + 1) * NPC, :] for k in (p, p + 1)], axis=1
        ).astype(BF16)
        both = jnp.dot(stacked, pair, preferred_element_type=F32)
        weight = jnp.concatenate(
            [jnp.broadcast_to(columns[:, k : k + 1], (QP, LANES)) for k in (p, p + 1)], axis=1
        )
        weighted = (weight * both[:QP]).astype(BF16)
        result = jnp.dot(basis_t, weighted, preferred_element_type=F32) + both[QP:]
        for k in (p, p + 1):
            out[k * NPC : (k + 1) * NPC, :] = result[:, (k - p) * LANES : (k - p + 1) * LANES]


def scatter(res, lists, cells, sums, batch):
    for p in range(0, GROUP, 2):
        for start in range(0, NPC, batch):
            moved = []
            for k in (p, p + 1):
                for j in range(start, start + batch):
                    row = pl.ds(lists[j][cells[k]], 1)
                    total = sums[k - p][row, :] + res[k * NPC + j : k * NPC + j + 1, :]
                    moved.append((k - p, row, total))
            for which, row, total in moved:
                sums[which][row, :] = total


def cells_of(group):
    return [group * GROUP + k for k in range(GROUP)]


def sweep(begin, end, repeated, src, lists, pot, stacked_ref, basis_t_ref, sums, vals, ress):
    def mult(slot, group, stacked, basis_t):
        multiply(vals[slot], pot, group * GROUP, stacked, basis_t, ress[slot])

    def two(i, _):
        first = 2 * i

        @pl.when(i >= 0)
        def _():
            scatter(ress[1], lists, cells_of(jnp.maximum(first - 1, 2 * begin)), sums, BATCH)
            mult(0, first, stacked_ref[...], basis_t_ref[...])
            gather(src, lists, cells_of(first + 1), vals[1])

        @pl.when(first >= 0)
        def _():
            scatter(ress[0], lists, cells_of(first), sums, BATCH)
            mult(1, first + 1, stacked_ref[...], basis_t_ref[...])
            gather(src, lists, cells_of(jnp.minimum(first + 2, 2 * end - 1)), vals[0])

        return 0

    @pl.when((end > begin) & (repeated == 0))
    def _():
        ress[1][...] = jnp.zeros_like(ress[1])
        gather(src, lists, cells_of(2 * begin), vals[0])
        lax.fori_loop(begin, end, two, 0)
        scatter(ress[1], lists, cells_of(2 * end - 1), sums, BATCH)

    @pl.when((end > begin) & (repeated != 0))
    def _():
        def one(i, _):
            gather(src, lists, cells_of(i), vals[0])
            mult(0, i, stacked_ref[...], basis_t_ref[...])
            scatter(ress[0], lists, cells_of(i), sums, 1)
            return 0

        lax.fori_loop(2 * begin, 2 * end, one, 0)


def start_kernel(edge_count, early, conn, states, mass_rows, *refs):
    given, refs = refs[:early], refs[early:]
    mass, kept, src, sum_a, sum_b, states_edge, mass_edge, sent = refs[:8]
    lists, held, arrived = refs[8 : 8 + NPC], refs[8 + NPC : 13 + NPC], refs[13 + NPC]
    edge = held[0]
    copies = [
        pltpu.make_async_copy(conn.at[pl.ds(j * STRIDE, STRIDE)], lists[j], arrived.at[j])
        for j in range(NPC)
    ]
    copies += [
        pltpu.make_async_copy(source, ref, arrived.at[NPC + n])
        for n, (source, ref) in enumerate(zip(given, held))
    ]
    for copy in copies:
        copy.start()
    nodes = states.shape[0]
    padded = kept.shape[0]
    whole = nodes // ROWS * ROWS

    def widen(rows):
        sum_a[rows, :] = states[rows, :].astype(F32)

    by_rows(whole, widen)
    if whole < padded:
        sum_a[whole:padded, :] = jnp.zeros((padded - whole, LANES), F32)
        sum_a[whole:nodes, :] = states[whole:nodes, :].astype(F32)

    def scale(columns, k, first):
        rows = pl.ds(pl.multiple_of(first + k * ROWS, ROWS), ROWS)
        column = jnp.broadcast_to(columns[:, k : k + 1], (ROWS, LANES))
        value = sum_a[rows, :]
        mass[rows, :] = column
        kept[rows, :] = value.astype(BF16)
        src[rows, :] = (column * value).astype(BF16).astype(F32)

    def eight(i, _):
        columns = mass_rows[pl.ds(pl.multiple_of(i * 8, 8), 8), :].T
        for k in range(8):
            scale(columns, k, i * (8 * ROWS))
        return 0

    chunks = padded // ROWS
    lax.fori_loop(0, chunks // 8, eight, 0)
    if chunks % 8:
        columns = mass_rows[chunks // 8 * 8 : chunks // 8 * 8 + 8, :].T
        for k in range(chunks % 8):
            scale(columns, k, chunks // 8 * 8 * ROWS)
    tail = states_edge.shape[0] - 8
    states_edge[tail:, :] = jnp.zeros((8, LANES), F32)
    mass_edge[tail:, :] = jnp.zeros((8, LANES), F32)

    for copy in copies:
        copy.wait()

    def take(i):
        row = pl.ds(edge[i], 1)
        states_edge[pl.ds(i, 1), :] = sum_a[row, :]
        mass_edge[pl.ds(i, 1), :] = mass[row, :]

    by_entries(edge_count, take)
    sent[...] = (mass_edge[...] * states_edge[...]).astype(BF16)
    src[padded:, :] = jnp.zeros((src.shape[0] - padded, LANES), F32)

    def clear(rows):
        sum_a[rows, :] = jnp.zeros((ROWS, LANES), F32)
        sum_b[rows, :] = jnp.zeros((ROWS, LANES), F32)

    by_rows(sum_a.shape[0], clear)


def cells_kernel(part, which, edge_count, padded, *refs):
    refs = list(refs)
    counts, pot, stacked, basis_t, src, sum_a, sum_b = refs[:7]
    lists, refs = refs[7 : 7 + NPC], refs[7 + NPC :]
    if part == 0 and which > 1:
        edge, scaled_edge = refs[:2]
        refs = refs[2:]
    if part == 1:
        ghost = refs.pop(0)
    sources = []
    if part == 2:
        edge = refs.pop(0)
        if which == 3:
            second_edge = refs.pop(0)
        loads = 3 if which == 2 else 2
        sources, refs = refs[:loads], refs[loads:]
    refs = refs[3:]
    if part == 1:
        outgoing = refs.pop(0)
    if part == 2:
        edge_sums, result = refs[:2]
        refs = refs[2:]
        if which == 3:
            second = refs.pop(0)
    val_a, val_b, res_a, res_b = refs[:4]
    refs = refs[4:]
    if part == 2:
        loaded, refs = refs[0], refs[1:]
        fetches = [
            pltpu.make_async_copy(source, ref, loaded.at[n])
            for n, (source, ref) in enumerate(zip(sources, refs))
        ]
    if part == 2:
        for fetch in fetches:
            fetch.start()
    if part == 0 and which > 1:

        def patch(i):
            src[pl.ds(edge[i], 1), :] = scaled_edge[pl.ds(i, 1), :]

        by_entries(edge_count, patch)
    if part == 1:
        src[padded : padded + ghost.shape[0], :] = ghost[...].astype(F32)

    split = counts[4] if which == 3 else counts[0]
    begin, end = ((0, split), (counts[1], counts[2]), (split, counts[1]))[part]
    sums = (sum_a, sum_b)
    sweep(
        begin,
        end,
        counts[3],
        src,
        lists,
        pot,
        stacked,
        basis_t,
        sums,
        (val_a, val_b),
        (res_a, res_b),
    )
    if part == 1:
        ghost_rows = slice(padded, padded + ghost.shape[0])
        outgoing[...] = (sum_a[ghost_rows, :] + sum_b[ghost_rows, :]).astype(BF16)
        blank = jnp.zeros(ghost.shape, F32)
        sum_a[ghost_rows, :] = blank
        sum_b[ghost_rows, :] = blank
    if part < 2:
        return

    for fetch in fetches:
        fetch.wait()
    mass, values = refs[:2]
    tail = edge_sums.shape[0] - 8
    edge_sums[tail:, :] = jnp.zeros((8, LANES), F32)

    def take(i):
        row = pl.ds(edge[i], 1)
        edge_sums[pl.ds(i, 1), :] = sum_a[row, :] + sum_b[row, :]
        if which == 3:
            sum_a[row, :] = jnp.zeros((1, LANES), F32)
            sum_b[row, :] = jnp.zeros((1, LANES), F32)

    by_entries(edge_count, take)

    def finish(rows):
        scale = mass[rows, :]
        image = scale * (sum_a[rows, :] + sum_b[rows, :])
        value = values[rows, :].astype(F32)
        if which == 3:
            refs[2][rows, :] = image.astype(BF16)
            src[rows, :] = value
            return
        if which == 1:
            after = ((image - CENTER * value) * INV_HALF).astype(BF16)
        else:
            start = refs[2][rows, :].astype(F32)
            after = (2.0 * INV_HALF * (image - CENTER * value) - start).astype(BF16)
        result[rows, :] = after
        src[rows, :] = (scale * after.astype(F32)).astype(BF16).astype(F32)
        sum_a[rows, :] = jnp.zeros((ROWS, LANES), F32)
        sum_b[rows, :] = jnp.zeros((ROWS, LANES), F32)

    by_rows(padded, finish)
    if which == 3:
        leaving = [
            pltpu.make_async_copy(refs[2], result.at[:, pl.ds(0, LANES)], loaded.at[0]),
            pltpu.make_async_copy(values, result.at[:, pl.ds(LANES, LANES)], loaded.at[1]),
        ]
        leaving[0].start()

        def blank(i):
            src[pl.ds(edge[i], 1), :] = jnp.zeros((1, LANES), F32)

        def fill(i):
            src[pl.ds(edge[i], 1), :] = second_edge[pl.ds(i, 1), :]

        def blanked(rows):
            values[rows, :] = src[rows, :].astype(BF16)

        def filled(rows):
            second[rows, :] = src[rows, :].astype(BF16)

        nodes = second.shape[0]
        by_entries(edge_count, blank)
        by_rows(padded, blanked)
        leaving[1].start()
        by_entries(edge_count, fill)
        whole = nodes // ROWS * ROWS
        by_rows(whole, filled)
        if whole < nodes:
            second[whole:nodes, :] = src[whole:nodes, :].astype(BF16)
        for copy in leaving:
            copy.wait()


def arrange(connectivity, potential, node_count, padded):
    cell_count = connectivity.shape[1]
    is_ghost = connectivity >= node_count
    late = jnp.any(is_ghost, axis=0).astype(F32)[None]
    before = jnp.triu(jnp.ones((cell_count, cell_count), F32), 1)
    ranks = jnp.dot(jnp.concatenate([late, 1.0 - late], 0), before, precision=EXACT)
    late_count = jnp.sum(late).astype(jnp.int32)
    turns = (cell_count - late_count + TURN - 1) // TURN
    late_turns = (late_count + TURN - 1) // TURN
    place = jnp.where(late[0] > 0, (turns * TURN).astype(F32) + ranks[0], ranks[1])
    slots = round_up(round_up(cell_count, TURN) + TURN, LANES)
    hot = (place[:, None] == jnp.arange(slots, dtype=F32)[None, :]).astype(F32)
    moved = jnp.dot(
        jnp.concatenate([connectivity.astype(F32), potential], 0), hot, precision=EXACT
    )
    index = jnp.round(moved[:NPC]).astype(jnp.int32)
    index = jnp.where(index >= node_count, index + (padded - node_count), index)
    used = jnp.sum(hot, axis=0) > 0
    spare = node_count + jnp.arange(NPC, dtype=jnp.int32)
    index = jnp.where(used[None, :], index, spare[:, None])
    lists = jnp.pad(index, ((0, 0), (0, STRIDE - slots))).reshape(-1)

    batched = jnp.where(is_ghost, connectivity, -1).reshape(NPC // BATCH, BATCH, cell_count)
    same = (batched[:, :, None] == batched[:, None, :]) & (batched[:, :, None] >= 0)
    apart = ~jnp.eye(BATCH, dtype=bool)[None, :, :, None]
    repeated = jnp.any(same & apart).astype(jnp.int32)
    counts = jnp.stack([turns // 2, turns, turns + late_turns, repeated, turns // 8])
    return lists, moved[NPC:], jnp.pad(counts, (0, LANES - counts.shape[0]))


def swap(value, dim, offset):
    step = 1
    for size in DIMS[dim + 1 :]:
        step *= size
    count, total = DIMS[dim], lax.axis_size("dom")
    pairs = []
    for source in range(total):
        digit = source // step % count
        pairs.append((source, source + ((digit + offset) % count - digit) * step))
    return lax.ppermute(value, "dom", pairs)


def choices(holder):
    here = lax.axis_index("dom")

    def digits(index):
        found = []
        for size in reversed(DIMS):
            found.append(index % size)
            index = index // size
        return found[::-1]

    mine, owner = digits(here), digits(holder)
    count = holder.shape[0]
    before = jnp.arange(count)[:, None] < jnp.arange(count)[None, :]

    def chosen(member, slots):
        rank = jnp.sum((member[:, None] & before).astype(jnp.int32), axis=0)
        return (member[None, :] & (rank[None, :] == jnp.arange(slots)[:, None])).astype(F32)

    column = (owner[0] == mine[0]) & (owner[3] == mine[3])
    plane_slots = min(count, DIMS[1] * CAP)
    for_plane = [
        chosen(column & (owner[2] == (mine[2] + k) % DIMS[2]), plane_slots)
        for k in range(DIMS[2])
    ]
    for_row = [
        chosen(column & (owner[2] == mine[2]) & (owner[1] == (mine[1] + k) % DIMS[1]), CAP)
        for k in range(DIMS[1])
    ]
    by_row = jnp.dot(jnp.concatenate(for_row, 0), for_plane[0].T, precision=EXACT)
    return jnp.concatenate(for_plane, 0), by_row


def to_owners(tiles, by_plane, by_row):
    plane_slots = by_row.shape[1]
    tiles = tiles + swap(tiles, 3, 1)
    tiles = tiles + swap(tiles, 0, 1)
    parts = jnp.dot(by_plane, tiles, precision=EXACT)
    parts = parts.reshape(DIMS[2], plane_slots, tiles.shape[1])
    total = parts[0]
    for arrived in [swap(parts[k], 2, k) for k in range(1, DIMS[2])]:
        total = total + arrived
    parts = jnp.dot(by_row, total, precision=EXACT)
    parts = parts.reshape(DIMS[1], CAP, tiles.shape[1])
    total = parts[0]
    for arrived in [swap(parts[k], 1, k) for k in range(1, DIMS[1])]:
        total = total + arrived
    return total


def local(states, mass_scale, potential, kinetic, basis_fn, connectivity, boundary, owners):
    node_count, state_count = states.shape
    edge_count = boundary.shape[0]
    padded = round_up(node_count + NPC, ROWS)
    edge_rows = round_up(edge_count + 7, 16)
    total_rows = round_up(padded + edge_rows, ROWS)

    wide = pltpu.VMEM((total_rows, LANES), F32)
    edge_shape = jax.ShapeDtypeStruct((edge_rows, LANES), F32)
    edge_half = jax.ShapeDtypeStruct((edge_rows, LANES), BF16)
    near_sums = pltpu.VMEM((edge_rows, LANES), F32)
    near_half = pltpu.VMEM((edge_rows, LANES), BF16)
    padded_half = jax.ShapeDtypeStruct((padded, LANES), BF16)
    both_half = jax.ShapeDtypeStruct((padded, 2 * LANES), BF16)
    whole_half = jax.ShapeDtypeStruct((node_count, LANES), BF16)

    mass_count = round_up(padded, 8 * ROWS)
    mass_rows = jnp.pad(mass_scale, (0, mass_count - node_count)).reshape(mass_count // ROWS, ROWS)
    stacked = jnp.concatenate([basis_fn, kinetic], 0)
    basis_t = basis_fn.T
    lists, pot, counts = arrange(connectivity, potential, node_count, padded)
    tile_rows = lax.axis_size("band") * state_count // TILE
    tile_cols = state_count // TILE
    tile_count = tile_rows * tile_cols
    holder = lax.dynamic_slice_in_dim(
        owners, lax.axis_index("band") * tile_cols, tile_cols, 1
    ).reshape(tile_count)
    by_plane, by_row = choices(holder)
    boundary = jnp.pad(boundary, (0, round_up(edge_count, STRIDE) - edge_count))
    first = lax.ppermute(states[:16], "band", [(0, 1), (1, 0)])
    early = (boundary, counts, pot, stacked, basis_t, by_plane, by_row, first)
    mass, kept, src, sum_a, sum_b, states_edge, mass_edge, sent, *lists = pl.pallas_call(
        functools.partial(start_kernel, edge_count, len(early)),
        out_shape=(jax.ShapeDtypeStruct((padded, LANES), F32), padded_half, wide, wide, wide)
        + (edge_shape, edge_shape, edge_half)
        + (pltpu.SMEM((STRIDE,), jnp.int32),) * NPC
        + tuple(pltpu.SMEM(given.shape, given.dtype) for given in early[:2])
        + tuple(pltpu.VMEM(given.shape, given.dtype) for given in early[2:5]),
        in_specs=[ANY, VMEM, VMEM] + [ANY] * len(early),
        out_specs=(VMEM,) * 8 + (SMEM,) * (NPC + 2) + (VMEM,) * 3,
        scratch_shapes=[pltpu.SemaphoreType.DMA((NPC + 5,))],
        compiler_params=params(SCOPED),
        cost_estimate=cost(10),
        name="start",
    )(lists, states, mass_rows, *early)
    lists, (edge, counts, pot, stacked, basis_t) = lists[:NPC], lists[NPC:]
    ghost = from_behind(sent, "dom", -1)
    block = pltpu.VMEM((GROUP * NPC, LANES), F32)

    def cells(part, which, held, specs, extra, outs, scratch=(), places=None):
        return pl.pallas_call(
            functools.partial(cells_kernel, part, which, edge_count, padded),
            out_shape=(wide, wide, wide) + outs,
            in_specs=[SMEM] + [VMEM] * 6 + [SMEM] * NPC + specs,
            out_specs=(VMEM,) * 3 + (places or (VMEM,) * len(outs)),
            input_output_aliases={4: 0, 5: 1, 6: 2},
            scratch_shapes=[block, block, block, block, *scratch],
            compiler_params=params(SCOPED),
            cost_estimate=cost(20),
            name=f"cells_{which}_{part}",
        )(counts, pot, stacked, basis_t, *held, *lists, *extra)

    def joined(edge_sums, outgoing):
        incoming = from_behind(outgoing, "dom", 1)
        return mass_edge * (edge_sums + incoming.astype(F32))

    def scaled(edge):
        return (mass_edge * edge).astype(BF16)

    loaded = pltpu.SemaphoreType.DMA((3,))
    mass_room = pltpu.VMEM((padded, LANES), F32)
    half_room = pltpu.VMEM((padded, LANES), BF16)
    held = cells(0, 1, (src, sum_a, sum_b), [], (), ())
    *held, outgoing = cells(1, 1, held, [VMEM], (ghost,), (near_half,))
    *held, sums, one = cells(
        2,
        1,
        held,
        [SMEM, ANY, ANY],
        (edge, mass, kept),
        (near_sums, padded_half),
        (loaded, mass_room, half_room),
    )
    one_edge = ((joined(sums, outgoing) - CENTER * states_edge) * INV_HALF).astype(BF16).astype(F32)

    sent = scaled(one_edge)
    ghost = from_behind(sent, "dom", -1)
    held = cells(0, 2, held, [SMEM, VMEM], (edge, sent.astype(F32)), ())
    *held, outgoing = cells(1, 2, held, [VMEM], (ghost,), (near_half,))
    *held, sums, two = cells(
        2,
        2,
        held,
        [SMEM, ANY, ANY, ANY],
        (edge, mass, one, kept),
        (near_sums, padded_half),
        (loaded, mass_room, half_room, half_room),
    )
    turned = [(0, 1), (1, 0)]
    two_half = (
        2.0 * INV_HALF * (joined(sums, outgoing) - CENTER * one_edge) - states_edge
    ).astype(BF16)
    two_edge = two_half.astype(F32)
    other_edge = lax.ppermute(two_half, "band", turned)

    sent = scaled(two_edge)
    ghost = from_behind(sent, "dom", -1)
    held = cells(0, 3, held, [SMEM, VMEM], (edge, sent.astype(F32)), ())
    ghost, two = lax.optimization_barrier((ghost, two))
    other = lax.ppermute(two, "band", turned)
    *held, outgoing = cells(1, 3, held, [VMEM], (ghost,), (near_half,))
    *held, sums, own, second = cells(
        2,
        3,
        held,
        [SMEM, VMEM, ANY, ANY],
        (edge, two_edge, mass, two),
        (near_sums, both_half, whole_half),
        (loaded, mass_room, half_room, half_room),
        (VMEM, ANY, VMEM),
    )
    image_edge = joined(sums, outgoing).astype(BF16)
    own_edge = jnp.concatenate([image_edge, two_half], 1)

    def project(columns, mine):
        return lax.dot_general(
            columns, mine, (((0,), (0,)), ((), ())), preferred_element_type=F32
        )

    inverse = 1.0 / (node_count * lax.axis_size("dom"))
    near = (project(two, own) + project(two_half, own_edge)) * inverse
    far = (project(other, own) + project(other_edge, own_edge)) * inverse
    lower = lax.axis_index("band") == 0
    pair = jnp.concatenate([jnp.where(lower, near, far), jnp.where(lower, far, near)], 0)

    tile_vals = (
        pair.reshape(tile_rows, TILE, 2, tile_cols, TILE)
        .transpose(0, 3, 2, 1, 4)
        .reshape(tile_count, 2 * TILE * TILE)
    )
    mine = to_owners(tile_vals, by_plane, by_row)
    return (second, mine.reshape(CAP, 1, 2, TILE * TILE))


def solution(mesh):
    return jax.shard_map(
        local,
        mesh=mesh,
        in_specs=(
            P("dom", "band"),
            P("dom"),
            P(None, "dom"),
            P(),
            P(),
            P(None, "dom"),
            P("dom"),
            P(),
        ),
        out_specs=(P("dom", "band"), P("dom", "band", None, None)),
        check_vma=False,
    )
```

```python
import functools

import jax
import jax.numpy as jnp
from jax import lax
from jax.experimental import pallas as pl
from jax.experimental.pallas import tpu as pltpu
from jax.sharding import PartitionSpec as P

NPC = 64
QP = 64
TILE = 32
CAP = 4
CENTER = 1.0
INV_HALF = 0.25
EXACT = lax.Precision.HIGHEST
DIMS = (2, 4, 4, 2)

LANES = 128
ROWS = 128
GROUP = 4
TURN = 2 * GROUP
BATCH = 8
SCOPED = 24
WINDOW = 384
STRIDE = 1024
F32 = jnp.float32
BF16 = jnp.bfloat16
VMEM = pl.BlockSpec(memory_space=pltpu.VMEM)
SMEM = pl.BlockSpec(memory_space=pltpu.SMEM)
ANY = pl.BlockSpec(memory_space=pl.ANY)
HBM = pl.BlockSpec(memory_space=pltpu.HBM)


def round_up(count, unit):
    return -(-count // unit) * unit


def from_behind(value, axis, steps):
    count = lax.axis_size(axis)
    initial, last = (max(0, -steps), min(count, count - steps))
    return lax.ppermute(value, axis, [(source, source + steps) for source in range(initial, last)])


def params(mebibytes):
    return pltpu.CompilerParams(vmem_limit_bytes=mebibytes << 20)


def cost(us):
    return pl.CostEstimate(flops=us * 10**9, bytes_accessed=us * 10**6, transcendentals=0)


def by_rows(count, work):
    def step(i, _):
        work(pl.ds(pl.multiple_of(i * ROWS, ROWS), ROWS))
        return 0

    lax.fori_loop(0, count // ROWS, step, 0)


def by_entries(count, work):
    unroll = max(u for u in range(1, 65) if count % u == 0)

    def step(i, _):
        for j in range(unroll):
            work(i * unroll + j)
        return 0

    lax.fori_loop(0, count // unroll, step, 0)


def gather(src, lists, cells, out):
    for k, cell in enumerate(cells):
        for j in range(NPC):
            out[k * NPC + j : k * NPC + j + 1, :] = src[pl.ds(lists[j][cell], 1), :]


def multiply(vals, pot, base, stacked, basis_t, out):
    chunk = pl.multiple_of((base // LANES) * LANES, LANES)
    shift = lax.rem(LANES - lax.rem(base, LANES), LANES)
    columns = pltpu.roll(pot[:, pl.ds(chunk, LANES)], shift, 1)
    for p in range(0, GROUP, 2):
        pair = jnp.concatenate(
            [vals[k * NPC : (k + 1) * NPC, :] for k in (p, p + 1)], axis=1
        ).astype(BF16)
        both = jnp.dot(stacked, pair, preferred_element_type=F32)
        weight = jnp.concatenate(
            [jnp.broadcast_to(columns[:, k : k + 1], (QP, LANES)) for k in (p, p + 1)], axis=1
        )
        weighted = (weight * both[:QP]).astype(BF16)
        result = jnp.dot(basis_t, weighted, preferred_element_type=F32) + both[QP:]
        for k in (p, p + 1):
            out[k * NPC : (k + 1) * NPC, :] = result[:, (k - p) * LANES : (k - p + 1) * LANES]


def scatter(res, lists, cells, sums, batch):
    for p in range(0, GROUP, 2):
        for start in range(0, NPC, batch):
            moved = []
            for k in (p, p + 1):
                for j in range(start, start + batch):
                    row = pl.ds(lists[j][cells[k]], 1)
                    total = sums[k - p][row, :] + res[k * NPC + j : k * NPC + j + 1, :]
                    moved.append((k - p, row, total))
            for which, row, total in moved:
                sums[which][row, :] = total


def cells_of(group):
    return [group * GROUP + k for k in range(GROUP)]


def sweep(begin, end, repeated, src, lists, pot, stacked_ref, basis_t_ref, sums, vals, ress):
    def mult(slot, group, stacked, basis_t):
        multiply(vals[slot], pot, group * GROUP, stacked, basis_t, ress[slot])

    def two(i, _):
        first = 2 * i

        @pl.when(i >= 0)
        def _():
            scatter(ress[1], lists, cells_of(jnp.maximum(first - 1, 2 * begin)), sums, BATCH)
            mult(0, first, stacked_ref[...], basis_t_ref[...])
            gather(src, lists, cells_of(first + 1), vals[1])

        @pl.when(first >= 0)
        def _():
            scatter(ress[0], lists, cells_of(first), sums, BATCH)
            mult(1, first + 1, stacked_ref[...], basis_t_ref[...])
            gather(src, lists, cells_of(jnp.minimum(first + 2, 2 * end - 1)), vals[0])

        return 0

    @pl.when((end > begin) & (repeated == 0))
    def _():
        ress[1][...] = jnp.zeros_like(ress[1])
        gather(src, lists, cells_of(2 * begin), vals[0])
        lax.fori_loop(begin, end, two, 0)
        scatter(ress[1], lists, cells_of(2 * end - 1), sums, BATCH)

    @pl.when((end > begin) & (repeated != 0))
    def _():
        def one(i, _):
            gather(src, lists, cells_of(i), vals[0])
            mult(0, i, stacked_ref[...], basis_t_ref[...])
            scatter(ress[0], lists, cells_of(i), sums, 1)
            return 0

        lax.fori_loop(2 * begin, 2 * end, one, 0)


def start_kernel(edge_count, early, states, mass_rows, *refs):
    given, refs = refs[:early], refs[early:]
    mass, kept, states_edge, mass_edge, sent = refs[:5]
    held, wide, arrived = refs[5:10], refs[10], refs[11]
    edge = held[0]
    copies = [
        pltpu.make_async_copy(source, ref, arrived.at[n])
        for n, (source, ref) in enumerate(zip(given, held))
    ]
    for copy in copies:
        copy.start()
    nodes = states.shape[0]
    padded = kept.shape[0]
    whole = nodes // ROWS * ROWS

    def widen(rows):
        wide[rows, :] = states[rows, :].astype(F32)

    by_rows(whole, widen)
    if whole < padded:
        wide[whole:padded, :] = jnp.zeros((padded - whole, LANES), F32)
        wide[whole:nodes, :] = states[whole:nodes, :].astype(F32)

    def scale(columns, k, first):
        rows = pl.ds(pl.multiple_of(first + k * ROWS, ROWS), ROWS)
        column = jnp.broadcast_to(columns[:, k : k + 1], (ROWS, LANES))
        value = wide[rows, :]
        mass[rows, :] = column
        kept[rows, :] = value.astype(BF16)

    def eight(i, _):
        columns = mass_rows[pl.ds(pl.multiple_of(i * 8, 8), 8), :].T
        for k in range(8):
            scale(columns, k, i * (8 * ROWS))
        return 0

    chunks = padded // ROWS
    lax.fori_loop(0, chunks // 8, eight, 0)
    if chunks % 8:
        columns = mass_rows[chunks // 8 * 8 : chunks // 8 * 8 + 8, :].T
        for k in range(chunks % 8):
            scale(columns, k, chunks // 8 * 8 * ROWS)
    tail = states_edge.shape[0] - 8
    states_edge[tail:, :] = jnp.zeros((8, LANES), F32)
    mass_edge[tail:, :] = jnp.zeros((8, LANES), F32)

    for copy in copies:
        copy.wait()

    def take(i):
        row = pl.ds(edge[i], 1)
        states_edge[pl.ds(i, 1), :] = wide[row, :]
        mass_edge[pl.ds(i, 1), :] = mass[row, :]

    by_entries(edge_count, take)
    sent[...] = (mass_edge[...] * states_edge[...]).astype(BF16)


def cells_kernel(part, which, edge_count, padded, *refs):
    refs = list(refs)
    conn, counts, pot, stacked, basis_t = refs[:5]
    refs = refs[5:]
    first = part == 0 and which == 1
    if not first:
        src, sum_a, sum_b = refs[:3]
        refs = refs[3:]
    if part == 0 and which > 1:
        edge, scaled_edge = refs[:2]
        refs = refs[2:]
    if part == 1:
        ghost = refs.pop(0)
    sources = []
    if first:
        sources, refs = refs[:2], refs[2:]
    if part == 2:
        edge = refs.pop(0)
        if which == 3:
            second_edge = refs.pop(0)
        loads = 3 if which == 2 else 2
        sources, refs = refs[:loads], refs[loads:]
    if first:
        src, sum_a, sum_b = refs[:3]
    refs = refs[3:]
    if part == 1:
        outgoing = refs.pop(0)
    if part == 2:
        edge_sums, result = refs[:2]
        refs = refs[2:]
        if which == 3:
            second = refs.pop(0)
    val_a, val_b, res_a, res_b, arrived = refs[:5]
    lists, refs = refs[5 : 5 + NPC], refs[5 + NPC :]
    if first or part == 2:
        loaded, refs = refs[0], refs[1:]
        fetches = [
            pltpu.make_async_copy(source, ref, loaded.at[n])
            for n, (source, ref) in enumerate(zip(sources, refs))
        ]
    if first or part == 2:
        for fetch in fetches:
            fetch.start()
    split = counts[4] if which == 3 else counts[0]
    begin, end = ((0, split), (counts[1], counts[2]), (split, counts[1]))[part]
    slots = pot.shape[1]
    base = begin * TURN // LANES * LANES
    short = (end * TURN - base <= WINDOW) & (base + WINDOW <= slots)

    def list_copies(offset, size):
        return [
            pltpu.make_async_copy(
                conn.at[pl.ds(pl.multiple_of(offset + j * STRIDE, LANES), size)],
                lists[j].at[pl.ds(offset, size)],
                arrived.at[j],
            )
            for j in range(NPC)
        ]

    @pl.when(short)
    def _():
        for copy in list_copies(pl.multiple_of(base, LANES), WINDOW):
            copy.start()

    @pl.when(jnp.logical_not(short))
    def _():
        for copy in list_copies(0, slots):
            copy.start()

    if first:
        for fetch in fetches:
            fetch.wait()
        mass, values = refs

        def prepare(rows):
            scaled = (mass[rows, :] * values[rows, :].astype(F32)).astype(BF16)
            src[rows, :] = scaled.astype(F32)

        def clear(rows):
            sum_a[rows, :] = jnp.zeros((ROWS, LANES), F32)
            sum_b[rows, :] = jnp.zeros((ROWS, LANES), F32)

        by_rows(padded, prepare)
        by_rows(sum_a.shape[0], clear)
        src[padded:, :] = jnp.zeros((src.shape[0] - padded, LANES), F32)
    if part == 0 and which > 1:

        def patch(i):
            src[pl.ds(edge[i], 1), :] = scaled_edge[pl.ds(i, 1), :]

        by_entries(edge_count, patch)
    if part == 1:
        src[padded : padded + ghost.shape[0], :] = ghost[...].astype(F32)

    @pl.when(short)
    def _():
        for copy in list_copies(pl.multiple_of(base, LANES), WINDOW):
            copy.wait()

    @pl.when(jnp.logical_not(short))
    def _():
        for copy in list_copies(0, slots):
            copy.wait()

    sums = (sum_a, sum_b)
    sweep(
        begin,
        end,
        counts[3],
        src,
        lists,
        pot,
        stacked,
        basis_t,
        sums,
        (val_a, val_b),
        (res_a, res_b),
    )
    if part == 1:
        ghost_rows = slice(padded, padded + ghost.shape[0])
        outgoing[...] = (sum_a[ghost_rows, :] + sum_b[ghost_rows, :]).astype(BF16)
        blank = jnp.zeros(ghost.shape, F32)
        sum_a[ghost_rows, :] = blank
        sum_b[ghost_rows, :] = blank
    if part < 2:
        return

    for fetch in fetches:
        fetch.wait()
    mass, values = refs[:2]
    tail = edge_sums.shape[0] - 8
    edge_sums[tail:, :] = jnp.zeros((8, LANES), F32)

    def take(i):
        row = pl.ds(edge[i], 1)
        edge_sums[pl.ds(i, 1), :] = sum_a[row, :] + sum_b[row, :]
        if which == 3:
            sum_a[row, :] = jnp.zeros((1, LANES), F32)
            sum_b[row, :] = jnp.zeros((1, LANES), F32)

    by_entries(edge_count, take)

    def finish(rows):
        scale = mass[rows, :]
        image = scale * (sum_a[rows, :] + sum_b[rows, :])
        value = values[rows, :].astype(F32)
        if which == 3:
            refs[2][rows, :] = image.astype(BF16)
            src[rows, :] = value
            return
        if which == 1:
            after = ((image - CENTER * value) * INV_HALF).astype(BF16)
        else:
            start = refs[2][rows, :].astype(F32)
            after = (2.0 * INV_HALF * (image - CENTER * value) - start).astype(BF16)
        result[rows, :] = after
        src[rows, :] = (scale * after.astype(F32)).astype(BF16).astype(F32)
        sum_a[rows, :] = jnp.zeros((ROWS, LANES), F32)
        sum_b[rows, :] = jnp.zeros((ROWS, LANES), F32)

    by_rows(padded, finish)
    if which == 3:
        leaving = [
            pltpu.make_async_copy(refs[2], result.at[:, pl.ds(0, LANES)], loaded.at[0]),
            pltpu.make_async_copy(values, result.at[:, pl.ds(LANES, LANES)], loaded.at[1]),
        ]
        leaving[0].start()

        def blank(i):
            src[pl.ds(edge[i], 1), :] = jnp.zeros((1, LANES), F32)

        def fill(i):
            src[pl.ds(edge[i], 1), :] = second_edge[pl.ds(i, 1), :]

        def blanked(rows):
            values[rows, :] = src[rows, :].astype(BF16)

        def filled(rows):
            second[rows, :] = src[rows, :].astype(BF16)

        nodes = second.shape[0]
        by_entries(edge_count, blank)
        by_rows(padded, blanked)
        leaving[1].start()
        by_entries(edge_count, fill)
        whole = nodes // ROWS * ROWS
        by_rows(whole, filled)
        if whole < nodes:
            second[whole:nodes, :] = src[whole:nodes, :].astype(BF16)
        for copy in leaving:
            copy.wait()


def arrange(connectivity, potential, node_count, padded):
    cell_count = connectivity.shape[1]
    is_ghost = connectivity >= node_count
    late = jnp.any(is_ghost, axis=0).astype(F32)[None]
    before = jnp.triu(jnp.ones((cell_count, cell_count), F32), 1)
    ranks = jnp.dot(jnp.concatenate([late, 1.0 - late], 0), before, precision=EXACT)
    late_count = jnp.sum(late).astype(jnp.int32)
    turns = (cell_count - late_count + TURN - 1) // TURN
    late_turns = (late_count + TURN - 1) // TURN
    place = jnp.where(late[0] > 0, (turns * TURN).astype(F32) + ranks[0], ranks[1])
    slots = round_up(round_up(cell_count, TURN) + TURN, LANES)
    hot = (place[:, None] == jnp.arange(slots, dtype=F32)[None, :]).astype(F32)
    moved = jnp.dot(
        jnp.concatenate([connectivity.astype(F32), potential], 0), hot, precision=EXACT
    )
    index = jnp.round(moved[:NPC]).astype(jnp.int32)
    index = jnp.where(index >= node_count, index + (padded - node_count), index)
    used = jnp.sum(hot, axis=0) > 0
    spare = node_count + jnp.arange(NPC, dtype=jnp.int32)
    index = jnp.where(used[None, :], index, spare[:, None])
    lists = jnp.pad(index, ((0, 0), (0, STRIDE - slots))).reshape(-1)

    batched = jnp.where(is_ghost, connectivity, -1).reshape(NPC // BATCH, BATCH, cell_count)
    same = (batched[:, :, None] == batched[:, None, :]) & (batched[:, :, None] >= 0)
    apart = ~jnp.eye(BATCH, dtype=bool)[None, :, :, None]
    repeated = jnp.any(same & apart).astype(jnp.int32)
    counts = jnp.stack([turns // 2, turns, turns + late_turns, repeated, turns // 16])
    return lists, moved[NPC:], jnp.pad(counts, (0, LANES - counts.shape[0]))


def swap(value, dim, offset):
    step = 1
    for size in DIMS[dim + 1 :]:
        step *= size
    count, total = DIMS[dim], lax.axis_size("dom")
    pairs = []
    for source in range(total):
        digit = source // step % count
        pairs.append((source, source + ((digit + offset) % count - digit) * step))
    return lax.ppermute(value, "dom", pairs)


def choices(holder):
    here = lax.axis_index("dom")

    def digits(index):
        found = []
        for size in reversed(DIMS):
            found.append(index % size)
            index = index // size
        return found[::-1]

    mine, owner = digits(here), digits(holder)
    count = holder.shape[0]
    before = jnp.arange(count)[:, None] < jnp.arange(count)[None, :]

    def chosen(member, slots):
        rank = jnp.sum((member[:, None] & before).astype(jnp.int32), axis=0)
        return (member[None, :] & (rank[None, :] == jnp.arange(slots)[:, None])).astype(F32)

    column = (owner[0] == mine[0]) & (owner[3] == mine[3])
    plane_slots = min(count, DIMS[1] * CAP)
    for_plane = [
        chosen(column & (owner[2] == (mine[2] + k) % DIMS[2]), plane_slots)
        for k in range(DIMS[2])
    ]
    for_row = [
        chosen(column & (owner[2] == mine[2]) & (owner[1] == (mine[1] + k) % DIMS[1]), CAP)
        for k in range(DIMS[1])
    ]
    by_row = jnp.dot(jnp.concatenate(for_row, 0), for_plane[0].T, precision=EXACT)
    return jnp.concatenate(for_plane, 0), by_row


def to_owners(tiles, by_plane, by_row):
    plane_slots = by_row.shape[1]
    tiles = tiles + swap(tiles, 3, 1)
    tiles = tiles + swap(tiles.astype(BF16), 0, 1).astype(F32)
    parts = jnp.dot(by_plane, tiles, precision=EXACT)
    parts = parts.reshape(DIMS[2], plane_slots, tiles.shape[1])
    total = parts[0]
    for arrived in [swap(parts[k].astype(BF16), 2, k) for k in range(1, DIMS[2])]:
        total = total + arrived.astype(F32)
    parts = jnp.dot(by_row, total, precision=EXACT)
    parts = parts.reshape(DIMS[1], CAP, tiles.shape[1])
    total = parts[0]
    for arrived in [swap(parts[k].astype(BF16), 1, k) for k in range(1, DIMS[1])]:
        total = total + arrived.astype(F32)
    return total


def local(states, mass_scale, potential, kinetic, basis_fn, connectivity, boundary, owners):
    node_count, state_count = states.shape
    edge_count = boundary.shape[0]
    padded = round_up(node_count + NPC, ROWS)
    edge_rows = round_up(edge_count + 7, 16)
    total_rows = round_up(padded + edge_rows, ROWS)

    wide = pltpu.VMEM((total_rows, LANES), F32)
    edge_shape = jax.ShapeDtypeStruct((edge_rows, LANES), F32)
    edge_half = jax.ShapeDtypeStruct((edge_rows, LANES), BF16)
    near_sums = pltpu.VMEM((edge_rows, LANES), F32)
    near_half = pltpu.VMEM((edge_rows, LANES), BF16)
    padded_half = jax.ShapeDtypeStruct((padded, LANES), BF16)
    both_half = jax.ShapeDtypeStruct((padded, 2 * LANES), BF16)
    whole_half = jax.ShapeDtypeStruct((node_count, LANES), BF16)

    mass_count = round_up(padded, 8 * ROWS)
    mass_rows = jnp.pad(mass_scale, (0, mass_count - node_count)).reshape(mass_count // ROWS, ROWS)
    stacked = jnp.concatenate([basis_fn, kinetic], 0)
    basis_t = basis_fn.T
    lists, pot, counts = arrange(connectivity, potential, node_count, padded)
    boundary = jnp.pad(boundary, (0, round_up(edge_count, STRIDE) - edge_count))
    tile_rows = lax.axis_size("band") * state_count // TILE
    tile_cols = state_count // TILE
    tile_count = tile_rows * tile_cols
    holder = lax.dynamic_slice_in_dim(
        owners, lax.axis_index("band") * tile_cols, tile_cols, 1
    ).reshape(tile_count)
    by_plane, by_row = choices(holder)
    together = lax.ppermute(states[:16], "band", [(0, 1), (1, 0)])
    early = (boundary, counts, pot, stacked, basis_t, by_plane, by_row, together)
    mass, kept, states_edge, mass_edge, sent, *kept_small = pl.pallas_call(
        functools.partial(start_kernel, edge_count, len(early)),
        out_shape=(pltpu.HBM((padded, LANES), F32), pltpu.HBM((padded, LANES), BF16))
        + (edge_shape, edge_shape, edge_half)
        + tuple(pltpu.SMEM(given.shape, given.dtype) for given in early[:2])
        + tuple(pltpu.VMEM(given.shape, given.dtype) for given in early[2:5]),
        in_specs=[VMEM, VMEM] + [ANY] * len(early),
        out_specs=(VMEM,) * 5 + (SMEM,) * 2 + (VMEM,) * 3,
        scratch_shapes=[pltpu.VMEM((padded, LANES), F32), pltpu.SemaphoreType.DMA((5,))],
        compiler_params=params(SCOPED),
        cost_estimate=cost(10),
        name="start",
    )(states, mass_rows, *early)
    edge, counts, pot, stacked, basis_t = kept_small
    ghost = from_behind(sent, "dom", -1)
    block = pltpu.VMEM((GROUP * NPC, LANES), F32)

    def cells(part, which, held, specs, extra, outs, scratch=(), places=None):
        return pl.pallas_call(
            functools.partial(cells_kernel, part, which, edge_count, padded),
            out_shape=(wide, wide, wide) + outs,
            in_specs=[ANY, SMEM] + [VMEM] * (3 + len(held)) + specs,
            out_specs=(VMEM,) * 3 + (places or (VMEM,) * len(outs)),
            input_output_aliases={5: 0, 6: 1, 7: 2} if held else {},
            scratch_shapes=[block, block, block, block, pltpu.SemaphoreType.DMA((NPC,))]
            + [pltpu.SMEM((STRIDE,), jnp.int32)] * NPC
            + list(scratch),
            compiler_params=params(SCOPED),
            cost_estimate=cost(20),
            name=f"cells_{which}_{part}",
        )(lists, counts, pot, stacked, basis_t, *held, *extra)

    def joined(edge_sums, outgoing):
        incoming = from_behind(outgoing, "dom", 1)
        return mass_edge * (edge_sums + incoming.astype(F32))

    def scaled(edge):
        return (mass_edge * edge).astype(BF16)

    loaded = pltpu.SemaphoreType.DMA((3,))
    mass_room = pltpu.VMEM((padded, LANES), F32)
    half_room = pltpu.VMEM((padded, LANES), BF16)
    held = cells(0, 1, (), [HBM, HBM], (mass, kept), (), (loaded, mass_room, half_room))
    *held, outgoing = cells(1, 1, held, [VMEM], (ghost,), (near_half,))
    *held, sums, one = cells(
        2,
        1,
        held,
        [SMEM, HBM, HBM],
        (edge, mass, kept),
        (near_sums, padded_half),
        (loaded, mass_room, half_room),
    )
    one_edge = ((joined(sums, outgoing) - CENTER * states_edge) * INV_HALF).astype(BF16).astype(F32)

    sent = scaled(one_edge)
    ghost = from_behind(sent, "dom", -1)
    held = cells(0, 2, held, [SMEM, VMEM], (edge, sent.astype(F32)), ())
    *held, outgoing = cells(1, 2, held, [VMEM], (ghost,), (near_half,))
    *held, sums, two = cells(
        2,
        2,
        held,
        [SMEM, HBM, HBM, HBM],
        (edge, mass, one, kept),
        (near_sums, padded_half),
        (loaded, mass_room, half_room, half_room),
    )
    turned = [(0, 1), (1, 0)]
    two_half = (
        2.0 * INV_HALF * (joined(sums, outgoing) - CENTER * one_edge) - states_edge
    ).astype(BF16)
    two_edge = two_half.astype(F32)
    other_edge = lax.ppermute(two_half, "band", turned)

    sent = scaled(two_edge)
    ghost = from_behind(sent, "dom", -1)
    held = cells(0, 3, held, [SMEM, VMEM], (edge, sent.astype(F32)), ())
    ghost, two = lax.optimization_barrier((ghost, two))
    other = lax.ppermute(two, "band", turned)
    *held, outgoing = cells(1, 3, held, [VMEM], (ghost,), (near_half,))
    *held, sums, own, second = cells(
        2,
        3,
        held,
        [SMEM, VMEM, HBM, HBM],
        (edge, two_edge, mass, two),
        (near_sums, both_half, whole_half),
        (loaded, mass_room, half_room, half_room),
        (VMEM, ANY, VMEM),
    )
    image_edge = joined(sums, outgoing).astype(BF16)
    own_edge = jnp.concatenate([image_edge, two_half], 1)

    def project(columns, mine):
        return lax.dot_general(
            columns, mine, (((0,), (0,)), ((), ())), preferred_element_type=F32
        )

    inverse = 1.0 / (node_count * lax.axis_size("dom"))
    near_own, near_edge = lax.optimization_barrier((own, own_edge))
    near = (project(two, near_own) + project(two_half, near_edge)) * inverse
    far = (project(other, own) + project(other_edge, own_edge)) * inverse
    lower = lax.axis_index("band") == 0
    pair = jnp.concatenate([jnp.where(lower, near, far), jnp.where(lower, far, near)], 0)

    tile_vals = (
        pair.reshape(tile_rows, TILE, 2, tile_cols, TILE)
        .transpose(0, 3, 2, 1, 4)
        .reshape(tile_count, 2 * TILE * TILE)
    )
    mine = to_owners(tile_vals, by_plane, by_row)
    return (second, mine.reshape(CAP, 1, 2, TILE * TILE))


def solution(mesh):
    return jax.shard_map(
        local,
        mesh=mesh,
        in_specs=(
            P("dom", "band"),
            P("dom"),
            P(None, "dom"),
            P(),
            P(),
            P(None, "dom"),
            P("dom"),
            P(),
        ),
        out_specs=(P("dom", "band"), P("dom", "band", None, None)),
        check_vma=False,
    )
```

```python
import functools

import jax
import jax.numpy as jnp
from jax import lax
from jax.experimental import pallas as pl
from jax.experimental.pallas import tpu as pltpu
from jax.sharding import PartitionSpec as P

NPC = 64
QP = 64
TILE = 32
CAP = 4
CENTER = 1.0
INV_HALF = 0.25
EXACT = lax.Precision.HIGHEST
DIMS = (2, 4, 4, 2)

LANES = 128
ROWS = 128
GROUP = 4
TURN = 2 * GROUP
BATCH = 8
SCOPED = 24
WINDOWS = (256, 384)
STRIDE = 1024
F32 = jnp.float32
BF16 = jnp.bfloat16
VMEM = pl.BlockSpec(memory_space=pltpu.VMEM)
SMEM = pl.BlockSpec(memory_space=pltpu.SMEM)
ANY = pl.BlockSpec(memory_space=pl.ANY)
HBM = pl.BlockSpec(memory_space=pltpu.HBM)


def round_up(count, unit):
    return -(-count // unit) * unit


def from_behind(value, axis, steps):
    count = lax.axis_size(axis)
    initial, last = (max(0, -steps), min(count, count - steps))
    return lax.ppermute(value, axis, [(source, source + steps) for source in range(initial, last)])


def params(mebibytes):
    return pltpu.CompilerParams(vmem_limit_bytes=mebibytes << 20)


def cost(us):
    return pl.CostEstimate(flops=us * 10**9, bytes_accessed=us * 10**6, transcendentals=0)


def by_rows(count, work):
    def step(i, _):
        work(pl.ds(pl.multiple_of(i * ROWS, ROWS), ROWS))
        return 0

    lax.fori_loop(0, count // ROWS, step, 0)


def by_entries(count, work):
    unroll = max(u for u in range(1, 65) if count % u == 0)

    def step(i, _):
        for j in range(unroll):
            work(i * unroll + j)
        return 0

    lax.fori_loop(0, count // unroll, step, 0)


def gather(src, lists, cells, out):
    for k, cell in enumerate(cells):
        for j in range(NPC):
            out[k * NPC + j : k * NPC + j + 1, :] = src[pl.ds(lists[j][cell], 1), :]


def multiply(vals, pot, base, stacked, basis_t, out):
    chunk = pl.multiple_of((base // LANES) * LANES, LANES)
    shift = lax.rem(LANES - lax.rem(base, LANES), LANES)
    columns = pltpu.roll(pot[:, pl.ds(chunk, LANES)], shift, 1)
    for p in range(0, GROUP, 2):
        pair = jnp.concatenate(
            [vals[k * NPC : (k + 1) * NPC, :] for k in (p, p + 1)], axis=1
        ).astype(BF16)
        both = jnp.dot(stacked, pair, preferred_element_type=F32)
        weight = jnp.concatenate(
            [jnp.broadcast_to(columns[:, k : k + 1], (QP, LANES)) for k in (p, p + 1)], axis=1
        )
        weighted = (weight * both[:QP]).astype(BF16)
        result = jnp.dot(basis_t, weighted, preferred_element_type=F32) + both[QP:]
        for k in (p, p + 1):
            out[k * NPC : (k + 1) * NPC, :] = result[:, (k - p) * LANES : (k - p + 1) * LANES]


def scatter(res, lists, cells, sums, batch):
    for p in range(0, GROUP, 2):
        for start in range(0, NPC, batch):
            moved = []
            for k in (p, p + 1):
                for j in range(start, start + batch):
                    row = pl.ds(lists[j][cells[k]], 1)
                    total = sums[k - p][row, :] + res[k * NPC + j : k * NPC + j + 1, :]
                    moved.append((k - p, row, total))
            for which, row, total in moved:
                sums[which][row, :] = total


def cells_of(group):
    return [group * GROUP + k for k in range(GROUP)]


def sweep(begin, end, repeated, src, lists, pot, stacked_ref, basis_t_ref, sums, vals, ress):
    def mult(slot, group, stacked, basis_t):
        multiply(vals[slot], pot, group * GROUP, stacked, basis_t, ress[slot])

    def two(i, _):
        first = 2 * i

        @pl.when(i >= 0)
        def _():
            scatter(ress[1], lists, cells_of(jnp.maximum(first - 1, 2 * begin)), sums, BATCH)
            mult(0, first, stacked_ref[...], basis_t_ref[...])
            gather(src, lists, cells_of(first + 1), vals[1])

        @pl.when(first >= 0)
        def _():
            scatter(ress[0], lists, cells_of(first), sums, BATCH)
            mult(1, first + 1, stacked_ref[...], basis_t_ref[...])
            gather(src, lists, cells_of(jnp.minimum(first + 2, 2 * end - 1)), vals[0])

        return 0

    @pl.when((end > begin) & (repeated == 0))
    def _():
        ress[1][...] = jnp.zeros_like(ress[1])
        gather(src, lists, cells_of(2 * begin), vals[0])
        lax.fori_loop(begin, end, two, 0)
        scatter(ress[1], lists, cells_of(2 * end - 1), sums, BATCH)

    @pl.when((end > begin) & (repeated != 0))
    def _():
        def one(i, _):
            gather(src, lists, cells_of(i), vals[0])
            mult(0, i, stacked_ref[...], basis_t_ref[...])
            scatter(ress[0], lists, cells_of(i), sums, 1)
            return 0

        lax.fori_loop(2 * begin, 2 * end, one, 0)


def start_kernel(edge_count, early, states, mass_rows, *refs):
    given, refs = refs[:early], refs[early:]
    mass, kept, states_edge, mass_edge, sent = refs[:5]
    held, wide, arrived = refs[5:10], refs[10], refs[11]
    edge = held[0]
    copies = [
        pltpu.make_async_copy(source, ref, arrived.at[n])
        for n, (source, ref) in enumerate(zip(given, held))
    ]
    for copy in copies:
        copy.start()
    nodes = states.shape[0]
    padded = kept.shape[0]
    whole = nodes // ROWS * ROWS

    def widen(rows):
        wide[rows, :] = states[rows, :].astype(F32)

    by_rows(whole, widen)
    if whole < padded:
        wide[whole:padded, :] = jnp.zeros((padded - whole, LANES), F32)
        wide[whole:nodes, :] = states[whole:nodes, :].astype(F32)

    def scale(columns, k, first):
        rows = pl.ds(pl.multiple_of(first + k * ROWS, ROWS), ROWS)
        column = jnp.broadcast_to(columns[:, k : k + 1], (ROWS, LANES))
        value = wide[rows, :]
        mass[rows, :] = column
        kept[rows, :] = value.astype(BF16)

    def eight(i, _):
        columns = mass_rows[pl.ds(pl.multiple_of(i * 8, 8), 8), :].T
        for k in range(8):
            scale(columns, k, i * (8 * ROWS))
        return 0

    chunks = padded // ROWS
    lax.fori_loop(0, chunks // 8, eight, 0)
    if chunks % 8:
        columns = mass_rows[chunks // 8 * 8 : chunks // 8 * 8 + 8, :].T
        for k in range(chunks % 8):
            scale(columns, k, chunks // 8 * 8 * ROWS)
    tail = states_edge.shape[0] - 8
    states_edge[tail:, :] = jnp.zeros((8, LANES), F32)
    mass_edge[tail:, :] = jnp.zeros((8, LANES), F32)

    for copy in copies:
        copy.wait()

    def take(i):
        row = pl.ds(edge[i], 1)
        states_edge[pl.ds(i, 1), :] = wide[row, :]
        mass_edge[pl.ds(i, 1), :] = mass[row, :]

    by_entries(edge_count, take)
    sent[...] = (mass_edge[...] * states_edge[...]).astype(BF16)


def cells_kernel(part, which, edge_count, padded, *refs):
    refs = list(refs)
    conn, counts, pot, stacked, basis_t = refs[:5]
    refs = refs[5:]
    first = part == 0 and which == 1
    if not first:
        src, sum_a, sum_b = refs[:3]
        refs = refs[3:]
    if part == 0 and which > 1:
        edge, scaled_edge = refs[:2]
        refs = refs[2:]
    if part == 1:
        ghost = refs.pop(0)
    sources = []
    if first:
        sources, refs = refs[:2], refs[2:]
    if part == 2:
        edge = refs.pop(0)
        if which == 3:
            second_edge = refs.pop(0)
        loads = 3 if which == 2 else 2
        sources, refs = refs[:loads], refs[loads:]
    if first:
        src, sum_a, sum_b = refs[:3]
    refs = refs[3:]
    if part == 1:
        outgoing = refs.pop(0)
    if part == 2:
        edge_sums, result = refs[:2]
        refs = refs[2:]
        if which == 3:
            second = refs.pop(0)
    val_a, val_b, res_a, res_b, arrived = refs[:5]
    lists, refs = refs[5 : 5 + NPC], refs[5 + NPC :]
    if first or part == 2:
        loaded, refs = refs[0], refs[1:]
        fetches = [
            pltpu.make_async_copy(source, ref, loaded.at[n])
            for n, (source, ref) in enumerate(zip(sources, refs))
        ]
    if first or part == 2:
        for fetch in fetches:
            fetch.start()
    split = counts[4] if which == 3 else counts[0]
    begin, end = ((0, split), (counts[1], counts[2]), (split, counts[1]))[part]
    slots = pot.shape[1]
    base = begin * TURN // LANES * LANES
    fits = [(end * TURN - base <= size) & (base + size <= slots) for size in WINDOWS]
    cases = [
        (fits[0], base, WINDOWS[0]),
        (jnp.logical_not(fits[0]) & fits[1], base, WINDOWS[1]),
        (jnp.logical_not(fits[0]) & jnp.logical_not(fits[1]), 0, slots),
    ]

    def list_copies(offset, size):
        return [
            pltpu.make_async_copy(
                conn.at[pl.ds(pl.multiple_of(offset + j * STRIDE, LANES), size)],
                lists[j].at[pl.ds(pl.multiple_of(offset, LANES), size)],
                arrived.at[j],
            )
            for j in range(NPC)
        ]

    for chosen, offset, size in cases:

        @pl.when(chosen & (end > begin))
        def _():
            for copy in list_copies(offset, size):
                copy.start()

    if first:
        for fetch in fetches:
            fetch.wait()
        mass, values = refs

        def prepare(rows):
            scaled = (mass[rows, :] * values[rows, :].astype(F32)).astype(BF16)
            src[rows, :] = scaled.astype(F32)

        def clear(rows):
            sum_a[rows, :] = jnp.zeros((ROWS, LANES), F32)
            sum_b[rows, :] = jnp.zeros((ROWS, LANES), F32)

        by_rows(padded, prepare)
        by_rows(sum_a.shape[0], clear)
        src[padded:, :] = jnp.zeros((src.shape[0] - padded, LANES), F32)
    if part == 0 and which > 1:

        def patch(i):
            src[pl.ds(edge[i], 1), :] = scaled_edge[pl.ds(i, 1), :]

        by_entries(edge_count, patch)
    if part == 1:
        src[padded : padded + ghost.shape[0], :] = ghost[...].astype(F32)

    for chosen, offset, size in cases:

        @pl.when(chosen & (end > begin))
        def _():
            for copy in list_copies(offset, size):
                copy.wait()

    sums = (sum_a, sum_b)
    sweep(
        begin,
        end,
        counts[3],
        src,
        lists,
        pot,
        stacked,
        basis_t,
        sums,
        (val_a, val_b),
        (res_a, res_b),
    )
    if part == 1:
        ghost_rows = slice(padded, padded + ghost.shape[0])
        outgoing[...] = (sum_a[ghost_rows, :] + sum_b[ghost_rows, :]).astype(BF16)
        blank = jnp.zeros(ghost.shape, F32)
        sum_a[ghost_rows, :] = blank
        sum_b[ghost_rows, :] = blank
    if part < 2:
        return

    for fetch in fetches:
        fetch.wait()
    mass, values = refs[:2]
    tail = edge_sums.shape[0] - 8
    edge_sums[tail:, :] = jnp.zeros((8, LANES), F32)

    def take(i):
        row = pl.ds(edge[i], 1)
        edge_sums[pl.ds(i, 1), :] = sum_a[row, :] + sum_b[row, :]
        if which == 3:
            sum_a[row, :] = jnp.zeros((1, LANES), F32)
            sum_b[row, :] = jnp.zeros((1, LANES), F32)

    by_entries(edge_count, take)

    def finish(rows):
        scale = mass[rows, :]
        image = scale * (sum_a[rows, :] + sum_b[rows, :])
        value = values[rows, :].astype(F32)
        if which == 3:
            refs[2][rows, :] = image.astype(BF16)
            src[rows, :] = value
            return
        if which == 1:
            after = ((image - CENTER * value) * INV_HALF).astype(BF16)
        else:
            start = refs[2][rows, :].astype(F32)
            after = (2.0 * INV_HALF * (image - CENTER * value) - start).astype(BF16)
        result[rows, :] = after
        src[rows, :] = (scale * after.astype(F32)).astype(BF16).astype(F32)
        sum_a[rows, :] = jnp.zeros((ROWS, LANES), F32)
        sum_b[rows, :] = jnp.zeros((ROWS, LANES), F32)

    by_rows(padded, finish)
    if which == 3:
        leaving = [
            pltpu.make_async_copy(refs[2], result.at[:, pl.ds(0, LANES)], loaded.at[0]),
            pltpu.make_async_copy(values, result.at[:, pl.ds(LANES, LANES)], loaded.at[1]),
        ]
        leaving[0].start()

        def blank(i):
            src[pl.ds(edge[i], 1), :] = jnp.zeros((1, LANES), F32)

        def fill(i):
            src[pl.ds(edge[i], 1), :] = second_edge[pl.ds(i, 1), :]

        def blanked(rows):
            values[rows, :] = src[rows, :].astype(BF16)

        def filled(rows):
            second[rows, :] = src[rows, :].astype(BF16)

        nodes = second.shape[0]
        by_entries(edge_count, blank)
        by_rows(padded, blanked)
        leaving[1].start()
        by_entries(edge_count, fill)
        whole = nodes // ROWS * ROWS
        by_rows(whole, filled)
        if whole < nodes:
            second[whole:nodes, :] = src[whole:nodes, :].astype(BF16)
        for copy in leaving:
            copy.wait()


def arrange(connectivity, potential, node_count, padded):
    cell_count = connectivity.shape[1]
    is_ghost = connectivity >= node_count
    late = jnp.any(is_ghost, axis=0).astype(F32)[None]
    before = jnp.triu(jnp.ones((cell_count, cell_count), F32), 1)
    ranks = jnp.dot(jnp.concatenate([late, 1.0 - late], 0), before, precision=EXACT)
    late_count = jnp.sum(late).astype(jnp.int32)
    turns = (cell_count - late_count + TURN - 1) // TURN
    late_turns = (late_count + TURN - 1) // TURN
    place = jnp.where(late[0] > 0, (turns * TURN).astype(F32) + ranks[0], ranks[1])
    slots = round_up(round_up(cell_count, TURN) + TURN, LANES)
    hot = (place[:, None] == jnp.arange(slots, dtype=F32)[None, :]).astype(F32)
    moved = jnp.dot(
        jnp.concatenate([connectivity.astype(F32), potential], 0), hot, precision=EXACT
    )
    index = jnp.round(moved[:NPC]).astype(jnp.int32)
    index = jnp.where(index >= node_count, index + (padded - node_count), index)
    used = jnp.sum(hot, axis=0) > 0
    spare = node_count + jnp.arange(NPC, dtype=jnp.int32)
    index = jnp.where(used[None, :], index, spare[:, None])
    lists = jnp.pad(index, ((0, 0), (0, STRIDE - slots))).reshape(-1)

    batched = jnp.where(is_ghost, connectivity, -1).reshape(NPC // BATCH, BATCH, cell_count)
    same = (batched[:, :, None] == batched[:, None, :]) & (batched[:, :, None] >= 0)
    apart = ~jnp.eye(BATCH, dtype=bool)[None, :, :, None]
    repeated = jnp.any(same & apart).astype(jnp.int32)
    counts = jnp.stack([turns // 2, turns, turns + late_turns, repeated, 0 * turns])
    return lists, moved[NPC:], jnp.pad(counts, (0, LANES - counts.shape[0]))


def swap(value, dim, offset):
    step = 1
    for size in DIMS[dim + 1 :]:
        step *= size
    count, total = DIMS[dim], lax.axis_size("dom")
    pairs = []
    for source in range(total):
        digit = source // step % count
        pairs.append((source, source + ((digit + offset) % count - digit) * step))
    return lax.ppermute(value, "dom", pairs)


def choices(holder):
    here = lax.axis_index("dom")

    def digits(index):
        found = []
        for size in reversed(DIMS):
            found.append(index % size)
            index = index // size
        return found[::-1]

    mine, owner = digits(here), digits(holder)
    count = holder.shape[0]
    before = jnp.arange(count)[:, None] < jnp.arange(count)[None, :]

    def chosen(member, slots):
        rank = jnp.sum((member[:, None] & before).astype(jnp.int32), axis=0)
        return (member[None, :] & (rank[None, :] == jnp.arange(slots)[:, None])).astype(F32)

    column = (owner[0] == mine[0]) & (owner[3] == mine[3])
    plane_slots = min(count, DIMS[1] * CAP)
    for_plane = [
        chosen(column & (owner[2] == (mine[2] + k) % DIMS[2]), plane_slots)
        for k in range(DIMS[2])
    ]
    for_row = [
        chosen(column & (owner[2] == mine[2]) & (owner[1] == (mine[1] + k) % DIMS[1]), CAP)
        for k in range(DIMS[1])
    ]
    by_row = jnp.dot(jnp.concatenate(for_row, 0), for_plane[0].T, precision=EXACT)
    return jnp.concatenate(for_plane, 0), by_row


def to_owners(tiles, by_plane, by_row):
    plane_slots = by_row.shape[1]
    tiles = tiles + swap(tiles, 3, 1)
    tiles = tiles + swap(tiles.astype(BF16), 0, 1).astype(F32)
    parts = jnp.dot(by_plane, tiles, precision=EXACT)
    parts = parts.reshape(DIMS[2], plane_slots, tiles.shape[1])
    total = parts[0]
    for arrived in [swap(parts[k].astype(BF16), 2, k) for k in range(1, DIMS[2])]:
        total = total + arrived.astype(F32)
    parts = jnp.dot(by_row, total, precision=EXACT)
    parts = parts.reshape(DIMS[1], CAP, tiles.shape[1])
    total = parts[0]
    for arrived in [swap(parts[k].astype(BF16), 1, k) for k in range(1, DIMS[1])]:
        total = total + arrived.astype(F32)
    return total


def local(states, mass_scale, potential, kinetic, basis_fn, connectivity, boundary, owners):
    node_count, state_count = states.shape
    edge_count = boundary.shape[0]
    padded = round_up(node_count + NPC, ROWS)
    edge_rows = round_up(edge_count + 7, 16)
    total_rows = round_up(padded + edge_rows, ROWS)

    wide = pltpu.VMEM((total_rows, LANES), F32)
    edge_shape = jax.ShapeDtypeStruct((edge_rows, LANES), F32)
    edge_half = jax.ShapeDtypeStruct((edge_rows, LANES), BF16)
    near_sums = pltpu.VMEM((edge_rows, LANES), F32)
    near_half = pltpu.VMEM((edge_rows, LANES), BF16)
    padded_half = jax.ShapeDtypeStruct((padded, LANES), BF16)
    both_half = jax.ShapeDtypeStruct((padded, 2 * LANES), BF16)
    whole_half = jax.ShapeDtypeStruct((node_count, LANES), BF16)

    mass_count = round_up(padded, 8 * ROWS)
    mass_rows = jnp.pad(mass_scale, (0, mass_count - node_count)).reshape(mass_count // ROWS, ROWS)
    stacked = jnp.concatenate([basis_fn, kinetic], 0)
    basis_t = basis_fn.T
    lists, pot, counts = arrange(connectivity, potential, node_count, padded)
    boundary = jnp.pad(boundary, (0, round_up(edge_count, STRIDE) - edge_count))
    tile_rows = lax.axis_size("band") * state_count // TILE
    tile_cols = state_count // TILE
    tile_count = tile_rows * tile_cols
    holder = lax.dynamic_slice_in_dim(
        owners, lax.axis_index("band") * tile_cols, tile_cols, 1
    ).reshape(tile_count)
    by_plane, by_row = choices(holder)
    together = lax.ppermute(states[:16], "band", [(0, 1), (1, 0)])
    early = (boundary, counts, pot, stacked, basis_t, by_plane, by_row, together)
    mass, kept, states_edge, mass_edge, sent, *kept_small = pl.pallas_call(
        functools.partial(start_kernel, edge_count, len(early)),
        out_shape=(pltpu.HBM((padded, LANES), F32), pltpu.HBM((padded, LANES), BF16))
        + (edge_shape, edge_shape, edge_half)
        + tuple(pltpu.SMEM(given.shape, given.dtype) for given in early[:2])
        + tuple(pltpu.VMEM(given.shape, given.dtype) for given in early[2:5]),
        in_specs=[VMEM, VMEM] + [ANY] * len(early),
        out_specs=(VMEM,) * 5 + (SMEM,) * 2 + (VMEM,) * 3,
        scratch_shapes=[pltpu.VMEM((padded, LANES), F32), pltpu.SemaphoreType.DMA((5,))],
        compiler_params=params(SCOPED),
        cost_estimate=cost(10),
        name="start",
    )(states, mass_rows, *early)
    edge, counts, pot, stacked, basis_t = kept_small
    ghost = from_behind(sent, "dom", -1)
    block = pltpu.VMEM((GROUP * NPC, LANES), F32)

    def cells(part, which, held, specs, extra, outs, scratch=(), places=None):
        return pl.pallas_call(
            functools.partial(cells_kernel, part, which, edge_count, padded),
            out_shape=(wide, wide, wide) + outs,
            in_specs=[ANY, SMEM] + [VMEM] * (3 + len(held)) + specs,
            out_specs=(VMEM,) * 3 + (places or (VMEM,) * len(outs)),
            input_output_aliases={5: 0, 6: 1, 7: 2} if held else {},
            scratch_shapes=[block, block, block, block, pltpu.SemaphoreType.DMA((NPC,))]
            + [pltpu.SMEM((STRIDE,), jnp.int32)] * NPC
            + list(scratch),
            compiler_params=params(SCOPED),
            cost_estimate=cost(20),
            name=f"cells_{which}_{part}",
        )(lists, counts, pot, stacked, basis_t, *held, *extra)

    def joined(edge_sums, outgoing):
        incoming = from_behind(outgoing, "dom", 1)
        return mass_edge * (edge_sums + incoming.astype(F32))

    def scaled(edge):
        return (mass_edge * edge).astype(BF16)

    loaded = pltpu.SemaphoreType.DMA((3,))
    mass_room = pltpu.VMEM((padded, LANES), F32)
    half_room = pltpu.VMEM((padded, LANES), BF16)
    held = cells(0, 1, (), [HBM, HBM], (mass, kept), (), (loaded, mass_room, half_room))
    *held, outgoing = cells(1, 1, held, [VMEM], (ghost,), (near_half,))
    *held, sums, one = cells(
        2,
        1,
        held,
        [SMEM, HBM, HBM],
        (edge, mass, kept),
        (near_sums, padded_half),
        (loaded, mass_room, half_room),
    )
    one_edge = ((joined(sums, outgoing) - CENTER * states_edge) * INV_HALF).astype(BF16).astype(F32)

    sent = scaled(one_edge)
    ghost = from_behind(sent, "dom", -1)
    held = cells(0, 2, held, [SMEM, VMEM], (edge, sent.astype(F32)), ())
    *held, outgoing = cells(1, 2, held, [VMEM], (ghost,), (near_half,))
    *held, sums, two = cells(
        2,
        2,
        held,
        [SMEM, HBM, HBM, HBM],
        (edge, mass, one, kept),
        (near_sums, padded_half),
        (loaded, mass_room, half_room, half_room),
    )
    turned = [(0, 1), (1, 0)]
    two_half = (
        2.0 * INV_HALF * (joined(sums, outgoing) - CENTER * one_edge) - states_edge
    ).astype(BF16)
    two_edge = two_half.astype(F32)
    other_edge = lax.ppermute(two_half, "band", turned)

    sent = scaled(two_edge)
    ghost = from_behind(sent, "dom", -1)
    held = cells(0, 3, held, [SMEM, VMEM], (edge, sent.astype(F32)), ())
    ghost, two = lax.optimization_barrier((ghost, two))
    other = lax.ppermute(two, "band", turned)
    *held, outgoing = cells(1, 3, held, [VMEM], (ghost,), (near_half,))
    *held, sums, own, second = cells(
        2,
        3,
        held,
        [SMEM, VMEM, HBM, HBM],
        (edge, two_edge, mass, two),
        (near_sums, both_half, whole_half),
        (loaded, mass_room, half_room, half_room),
        (VMEM, ANY, VMEM),
    )
    image_edge = joined(sums, outgoing).astype(BF16)
    own_edge = jnp.concatenate([image_edge, two_half], 1)

    def project(columns, mine):
        return lax.dot_general(
            columns, mine, (((0,), (0,)), ((), ())), preferred_element_type=F32
        )

    inverse = 1.0 / (node_count * lax.axis_size("dom"))
    near = (project(own, two) + project(own_edge, two_half)).T * inverse
    far = (project(other, own) + project(other_edge, own_edge)) * inverse
    lower = lax.axis_index("band") == 0
    pair = jnp.concatenate([jnp.where(lower, near, far), jnp.where(lower, far, near)], 0)

    tile_vals = (
        pair.reshape(tile_rows, TILE, 2, tile_cols, TILE)
        .transpose(0, 3, 2, 1, 4)
        .reshape(tile_count, 2 * TILE * TILE)
    )
    mine = to_owners(tile_vals, by_plane, by_row)
    return (second, mine.reshape(CAP, 1, 2, TILE * TILE))


def solution(mesh):
    return jax.shard_map(
        local,
        mesh=mesh,
        in_specs=(
            P("dom", "band"),
            P("dom"),
            P(None, "dom"),
            P(),
            P(),
            P(None, "dom"),
            P("dom"),
            P(),
        ),
        out_specs=(P("dom", "band"), P("dom", "band", None, None)),
        check_vma=False,
    )
```
